128 devices in a mesh: section: 2 (over core), dp: 64 (over z, y, x).
Axes of the slice: x: 4, y: 4, z: 4, core: 2. Of those that a mesh axis runs over, the one named last changes fastest.
Arguments:
- images: bfloat16 [128, 1024, 256], P('dp'), may hold values from -6 to 6
- queries: bfloat16 [128, 100, 256], P('dp'), may hold values from -6 to 6
- lengths: int32 [128], P('dp'), may hold values from 512 to 1024, as said below
- cotangent: float32 [128, 100, 256], P('dp'), may hold values from -6 to 6
- encoder_project: bfloat16 [256, 768], replicated, may hold values from -0.5 to 0.5
- encoder_output: bfloat16 [256, 256], replicated, may hold values from -1 to 1
- encoder_expand: bfloat16 [256, 2048], replicated, may hold values from -0.375 to 0.375
- encoder_shrink: bfloat16 [2048, 256], replicated, may hold values from -0.125 to 0.125
- encoder_gain: float32 [2, 256], replicated, may hold values from 0.1 to 1.9
- encoder_shift: float32 [2, 256], replicated, may hold values from -3 to 3
- decoder_project: bfloat16 [256, 768], replicated, may hold values from -0.5 to 0.5
- decoder_output: bfloat16 [256, 256], replicated, may hold values from -0.375 to 0.375
- cross_query: bfloat16 [256, 256], replicated, may hold values from -0.5 to 0.5
- cross_keyvalue: bfloat16 [256, 512], replicated, may hold values from -0.5 to 0.5
- cross_output: bfloat16 [256, 256], replicated, may hold values from -1 to 1
- decoder_expand: bfloat16 [256, 2048], replicated, may hold values from -0.375 to 0.375
- decoder_shrink: bfloat16 [2048, 256], replicated, may hold values from -0.125 to 0.125
- decoder_gain: float32 [3, 256], replicated, may hold values from 0.1 to 1.9
- decoder_shift: float32 [3, 256], replicated, may hold values from -3 to 3
Outputs:
- decoded: float32 [128, 100, 256], P('dp', None, 'section')
- images_grad: float32 [128, 1024, 256], P('dp', None, 'section')
- queries_grad: float32 [128, 100, 256], P('dp', None, 'section')
- encoder_project_grad: float32 [256, 768], replicated
- encoder_output_grad: float32 [256, 256], replicated
- encoder_expand_grad: float32 [256, 2048], replicated
- encoder_shrink_grad: float32 [2048, 256], replicated
- encoder_gain_grad: float32 [2, 256], replicated
- encoder_shift_grad: float32 [2, 256], replicated
- decoder_project_grad: float32 [256, 768], replicated
- decoder_output_grad: float32 [256, 256], replicated
- cross_query_grad: float32 [256, 256], replicated
- cross_keyvalue_grad: float32 [256, 512], replicated
- cross_output_grad: float32 [256, 256], replicated
- decoder_expand_grad: float32 [256, 2048], replicated
- decoder_shrink_grad: float32 [2048, 256], replicated
- decoder_gain_grad: float32 [3, 256], replicated
- decoder_shift_grad: float32 [3, 256], replicated
The draws below stay inside these ranges and needn't reach their ends.
Inputs may be any that keep to these rules, and one draw needn't show every extreme that they name: `lengths`: valid tokens of each image counted from its first row; the rest of its 1024 rows are padding.
All inputs are finite; a program needn't handle non-finite values.
Results may differ from the reference program's by a relative error of at most 0.03.
The reference program's roundings to bfloat16 on the way count: a program that leaves them out, or rounds other values in their place, can miss the bound.
Values may be sent and summed in bfloat16 or wider, within the bound.
No kernel may reach another device: no remote copies, remote signals or barrier semaphores. Data moves between devices by JAX's collectives and lax.ppermute only.
A program may use at most 192 MiB of HBM per device.

```python
import jax
import jax.numpy as jnp
from jax import lax

D = 256
H = 8
HD = 32
FF = 2048
QUERIES = 100
LMAX = 1024
IMAGES = 128


def draw_lengths(key, part):
    key = jax.random.fold_in(key, 7)
    length_key, chosen_key = jax.random.split(key)
    picked_lengths = jax.random.randint(length_key, (IMAGES,), LMAX // 2, LMAX + 1)
    chosen = jax.random.randint(chosen_key, (), 0, IMAGES)
    places = jnp.arange(IMAGES)
    picked_lengths = jnp.where(places == chosen, LMAX, picked_lengths)
    picked_lengths = jnp.where(places == (chosen + 1) % IMAGES, LMAX // 2, picked_lengths)
    return picked_lengths.astype(jnp.int32)


def block_scale(own_key, shape, pieces, low, largest):
    def one(dim, shards_of):
        draws = jax.random.uniform(jax.random.fold_in(jax.random.fold_in(own_key, 6), dim), (shards_of,), jnp.float32, low / len(pieces), largest / len(pieces))
        return jnp.repeat(jnp.exp(draws), shape[dim] // shards_of).reshape((-1,) + (1,) * (len(shape) - dim - 1))

    loudness = one(*pieces[0])
    for cut in pieces[1:]:
        loudness = loudness * one(*cut)
    return loudness


def bell_draw(rng, shape, spread, most, cuts=(), held_as=jnp.bfloat16):
    loudness = block_scale(rng, shape, cuts, -0.22, 0.18) if cuts else 1.0
    result = jax.random.normal(rng, shape, jnp.float32) * spread * loudness
    return jnp.minimum(jnp.maximum(result, -most), most).astype(held_as)


def setup_inputs(seed: int = 0) -> dict:
    splits = jax.random.split(jax.random.key(seed), 20)
    images = bell_draw(splits[0], (IMAGES, LMAX, D), 1.0, 6.0, ((0, 64),))
    queries = bell_draw(splits[1], (IMAGES, QUERIES, D), 1.0, 6.0, ((0, 64),))
    lengths = draw_lengths(jax.random.fold_in(splits[19], 71), 0)
    cotangent = bell_draw(splits[3], (IMAGES, QUERIES, D), 1.0, 6.0, ((0, 64),), jnp.float32)
    encoder_project = bell_draw(splits[4], (D, 3 * D), (D // 2) ** -0.5, 0.5)
    encoder_output = bell_draw(splits[5], (D, D), 32 ** -0.5, 1.0)
    encoder_expand = bell_draw(splits[6], (D, FF), D ** -0.5, 0.375)
    encoder_shrink = bell_draw(splits[7], (FF, D), FF ** -0.5, 0.125)
    encoder_gain = jnp.clip(1.0 + 0.18 * jax.random.normal(splits[8], (2, D), jnp.float32), 0.1, 1.9)
    encoder_shift = bell_draw(splits[9], (2, D), 0.5, 3.0, (), jnp.float32)
    decoder_project = bell_draw(splits[10], (D, 3 * D), (D // 2) ** -0.5, 0.5)
    decoder_output = bell_draw(splits[11], (D, D), D ** -0.5, 0.375)
    cross_query = bell_draw(splits[12], (D, D), (D // 2) ** -0.5, 0.5)
    cross_keyvalue = bell_draw(splits[13], (D, 2 * D), (D // 2) ** -0.5, 0.5)
    cross_output = bell_draw(splits[14], (D, D), 32 ** -0.5, 1.0)
    decoder_expand = bell_draw(splits[15], (D, FF), D ** -0.5, 0.375)
    decoder_shrink = bell_draw(splits[16], (FF, D), FF ** -0.5, 0.125)
    decoder_gain = jnp.clip(1.0 + 0.18 * jax.random.normal(splits[17], (3, D), jnp.float32), 0.1, 1.9)
    decoder_shift = bell_draw(splits[18], (3, D), 0.5, 3.0, (), jnp.float32)
    return dict(images=images, queries=queries, lengths=lengths, cotangent=cotangent, encoder_project=encoder_project, encoder_output=encoder_output, encoder_expand=encoder_expand, encoder_shrink=encoder_shrink, encoder_gain=encoder_gain, encoder_shift=encoder_shift, decoder_project=decoder_project, decoder_output=decoder_output, cross_query=cross_query, cross_keyvalue=cross_keyvalue, cross_output=cross_output, decoder_expand=decoder_expand, decoder_shrink=decoder_shrink, decoder_gain=decoder_gain, decoder_shift=decoder_shift)


EPSILON = 1e-05
NEGATIVE = -1e+30

@jax.custom_vjp
def low(v):
    return lax.optimization_barrier(v.astype(jnp.bfloat16)).astype(jnp.float32)

@jax.custom_vjp
def low_back(v):
    return v

def low_keep(v):
    return (low(v), None)

def low_pass(kept, grad):
    return (grad,)

def back_keep(v):
    return (v, None)

def back_low(kept, grad):
    return (low(grad),)
low.defvjp(low_keep, low_pass)
low_back.defvjp(back_keep, back_low)

def round_both(value):
    return low(low_back(value))

def multiply(left, right):
    return jnp.dot(left, right, precision=lax.Precision.HIGHEST, preferred_element_type=jnp.float32)

def norm_forward(totals, gain_row, shift_row):
    row_mean = lax.optimization_barrier(jnp.mean(totals, axis=-1, keepdims=True))
    centered = totals - row_mean
    variance = lax.optimization_barrier(jnp.mean(centered * centered, axis=-1, keepdims=True))
    return centered * lax.rsqrt(variance + EPSILON) * gain_row + shift_row

def attention(queries_in, keys_in, values_in, key_valid):
    row_count = queries_in.shape[0]
    key_count = keys_in.shape[0]
    query_split = queries_in.reshape(row_count, H, HD)
    keys_split = keys_in.reshape(key_count, H, HD)
    values_split = values_in.reshape(key_count, H, HD)
    scores = jnp.einsum('qhd,khd->hqk', query_split, keys_split, precision=lax.Precision.HIGHEST) * HD ** (-0.5)
    scores = low_back(scores)
    scores = jnp.where(key_valid[None, None, :], scores, NEGATIVE)
    row_peak = lax.optimization_barrier(jnp.max(scores, axis=-1, keepdims=True))
    exponent = jnp.exp(scores - row_peak)
    probabilities = exponent / lax.optimization_barrier(jnp.sum(exponent, axis=-1, keepdims=True))
    weights = low(probabilities)
    mixed_heads = jnp.einsum('hqk,khd->qhd', weights, values_split, precision=lax.Precision.HIGHEST)
    return mixed_heads.reshape(row_count, H * HD)

def encoder(image_rows, key_valid, weights):
    project_matrix, output_matrix, expand_matrix, shrink_matrix, gains, shifts = weights
    projected = round_both(multiply(image_rows, project_matrix))
    attended = round_both(attention(projected[:, :D], projected[:, D:2 * D], projected[:, 2 * D:], key_valid))
    branch_one = low_back(multiply(attended, output_matrix))
    normed = norm_forward(image_rows + branch_one, gains[0], shifts[0])
    hidden = low_back(multiply(low(normed), expand_matrix))
    active = low(jax.nn.gelu(hidden))
    branch_two = low_back(multiply(active, shrink_matrix))
    return round_both(norm_forward(normed + branch_two, gains[1], shifts[1]))

def decoder(query_rows, memory, key_valid, weights):
    project_matrix, output_matrix, query_matrix, pair_matrix, cross_matrix, expand_matrix, shrink_matrix, gains, shifts = weights
    all_valid = jnp.arange(QUERIES) < QUERIES
    projected = round_both(multiply(query_rows, project_matrix))
    attended = round_both(attention(projected[:, :D], projected[:, D:2 * D], projected[:, 2 * D:], all_valid))
    branch_one = low_back(multiply(attended, output_matrix))
    after_self = norm_forward(query_rows + branch_one, gains[0], shifts[0])
    cross_asked = round_both(multiply(low(after_self), query_matrix))
    cross_pairs = round_both(multiply(memory, pair_matrix))
    crossed = round_both(attention(cross_asked, cross_pairs[:, :D], cross_pairs[:, D:], key_valid))
    branch_two = low_back(multiply(crossed, cross_matrix))
    after_cross = norm_forward(after_self + branch_two, gains[1], shifts[1])
    hidden = low_back(multiply(low(after_cross), expand_matrix))
    active = low(jax.nn.gelu(hidden))
    branch_three = low_back(multiply(active, shrink_matrix))
    return norm_forward(after_cross + branch_three, gains[2], shifts[2])

def reference(images, queries, lengths, cotangent, encoder_project, encoder_output, encoder_expand, encoder_shrink, encoder_gain, encoder_shift, decoder_project, decoder_output, cross_query, cross_keyvalue, cross_output, decoder_expand, decoder_shrink, decoder_gain, decoder_shift):
    valid_all = jnp.arange(LMAX)[None, :] < lengths[:, None]
    weight_list = (encoder_project, encoder_output, encoder_expand, encoder_shrink, encoder_gain, encoder_shift, decoder_project, decoder_output, cross_query, cross_keyvalue, cross_output, decoder_expand, decoder_shrink, decoder_gain, decoder_shift)
    weight_values = tuple((member.astype(jnp.float32) for member in weight_list))

    def forward(images_float, queries_float, weights):
        encoder_weights = weights[:6]
        decoder_weights = weights[6:]

        def per_image(scan_carry, scan_item):
            image_rows, query_rows, key_valid = scan_item
            memory = encoder(image_rows, key_valid, encoder_weights)
            return (scan_carry, decoder(query_rows, memory, key_valid, decoder_weights))
        return lax.scan(jax.checkpoint(per_image), None, (images_float, queries_float, valid_all))[1]
    decoded, pullback = jax.vjp(forward, images.astype(jnp.float32), queries.astype(jnp.float32), weight_values)
    images_grad, queries_grad, weight_grads = pullback(cotangent.astype(jnp.float32))
    return (decoded, images_grad, queries_grad, weight_grads[0], weight_grads[1], weight_grads[2], weight_grads[3], weight_grads[4], weight_grads[5], weight_grads[6], weight_grads[7], weight_grads[8], weight_grads[9], weight_grads[10], weight_grads[11], weight_grads[12], weight_grads[13], weight_grads[14])
```

```python
import jax
import jax.numpy as jnp
from jax import lax
from jax.experimental import pallas as pl
from jax.experimental.pallas import tpu as pltpu
from jax.sharding import PartitionSpec as P

D = 256
H = 8
HD = 32
FF = 2048
QUERIES = 100
QP = 128
LANES = 128
LMAX = 1024
QB = 256
STEPS = LMAX // QB
HALF = STEPS // 2
FB = FF // STEPS
KT = 512
SHARE_MOST = 2.0**40

BF = jnp.bfloat16
F32 = jnp.float32
EPSILON = 1e-05
NEGATIVE = -1e30
SCALE = HD**-0.5
SCALE2 = SCALE * 1.4426950408889634
GELU_C = 0.7978845608028654
GELU_A = 0.044715
VMEM_LIMIT = 60 * 2**20


def dot(a, b):
    return lax.dot_general(a, b, (((1,), (0,)), ((), ())), preferred_element_type=F32)


def dot_nt(a, b):
    return lax.dot_general(a, b, (((1,), (1,)), ((), ())), preferred_element_type=F32)


def dot_tn(a, b):
    return lax.dot_general(a, b, (((0,), (0,)), ((), ())), preferred_element_type=F32)


def flip(a):
    return a.astype(F32).T


def norm_parts(totals):
    centered = totals - jnp.mean(totals, axis=-1, keepdims=True)
    rstd = lax.rsqrt(jnp.mean(centered * centered, axis=-1, keepdims=True) + EPSILON)
    return centered * rstd, rstd


def norm_back(grad, hat, rstd, gain_row):
    scaled = grad * gain_row
    inner = jnp.mean(scaled * hat, axis=-1, keepdims=True)
    grad_in = rstd * (scaled - jnp.mean(scaled, axis=-1, keepdims=True) - hat * inner)
    gain_grad = jnp.sum(grad * hat, axis=0, keepdims=True)
    shift_grad = jnp.sum(grad, axis=0, keepdims=True)
    return grad_in, gain_grad, shift_grad


def gelu_both(v):
    w = (GELU_C * GELU_A) * (v * v) + GELU_C
    half = 0.5 * jnp.tanh(v * w) + 0.5
    active = v * half
    slope = half + active * (1.0 - half) * (6.0 * w - 4.0 * GELU_C)
    return active, slope


def head_rows(n):
    return lax.broadcasted_iota(jnp.int32, (D, n), 0) >> 5


def head_lanes(n):
    return lax.broadcasted_iota(jnp.int32, (n, D), 1) >> 5


def stacked_rows(a):
    lanes = head_lanes(a.shape[0])
    zero = jnp.zeros_like(a)
    return jnp.concatenate([jnp.where(lanes == h, a, zero) for h in range(H)], axis=0)


def spread(rows, n):
    return jnp.concatenate(
        [jnp.broadcast_to(rows[h : h + 1, :], (HD, n)) for h in range(H)], axis=0
    )


def encoder_forward_kernel(
    lengths, x_ref, wp, wo, we, ws, gain, shift,
    e_ref, eo_ref, b1_ref, b2_ref, eg_ref, gp_ref, mem_ref, p_ref, r_ref,
    qt, vt, bias, ot,
):
    i = pl.program_id(0)
    s = section()

    @pl.when(i == 0)
    def _():
        e_ref[...] = dot(x_ref[s], wp[...]).astype(BF)
        qt[...] = flip(e_ref[:, :D]).astype(BF)
        vt[...] = flip(e_ref[:, 2 * D :]).astype(BF)
        rows = lax.broadcasted_iota(jnp.int32, (LMAX, 128), 0)
        bias[...] = jnp.where(rows < lengths[s], 0.0, NEGATIVE)

    here = pl.ds(pl.multiple_of(i * QB, QB), QB)
    q_block = qt[:, here]
    rows = head_rows(QB)
    zero = jnp.zeros_like(q_block)

    def mix(h, k):
        return dot(
            vt[h * HD : (h + 1) * HD, k : k + KT], p_ref[0, k : k + KT, h * QB : (h + 1) * QB]
        )

    def attend_unshifted():
        shares = [None] * H
        for h in range(H + 1):
            total = jnp.zeros((1, QB), F32)
            mixed = jnp.zeros((HD, QB), F32)
            for k in range(0, LMAX, KT):
                if h < H:
                    scores = dot(
                        e_ref[k : k + KT, D : 2 * D], jnp.where(rows == h, q_block, zero)
                    )
                    scores = scores * SCALE2
                    if k + KT > LMAX // 2:
                        scores = scores + bias[k : k + KT, 0:1]
                    exponent = jnp.exp2(scores)
                    total = total + jnp.sum(exponent, axis=0, keepdims=True)
                    p_ref[0, k : k + KT, h * QB : (h + 1) * QB] = exponent.astype(BF)
                if h > 0:
                    mixed = mixed + mix(h - 1, k)
            if h < H:
                shares[h] = 1.0 / total
                r_ref[0, h : h + 1, :] = shares[h]
            if h > 0:
                ot[(h - 1) * HD : h * HD, :] = mixed * shares[h - 1]

    def attend_shifted():
        for h in range(H):
            scores = dot(e_ref[:, D : 2 * D], jnp.where(rows == h, q_block, zero))
            scores = scores * SCALE2 + bias[:, 0:1]
            exponent = jnp.exp2(scores - jnp.max(scores, axis=0, keepdims=True))
            share = 1.0 / jnp.sum(exponent, axis=0, keepdims=True)
            p_ref[0, :, h * QB : (h + 1) * QB] = exponent.astype(BF)
            r_ref[0, h : h + 1, :] = share
            ot[h * HD : (h + 1) * HD, :] = (
                dot(vt[h * HD : (h + 1) * HD, :], exponent.astype(BF)) * share
            )

    def rest():
        attended = ot[...].T.astype(BF)
        eo_ref[...] = attended
        before_one = x_ref[s, here, :].astype(F32) + dot(attended, wo[...])
        b1_ref[...] = before_one
        hat = norm_parts(before_one)[0]
        normed = hat * gain[0:1, :] + shift[0:1, :]
        normed_low = normed.astype(BF)
        before_two = normed
        for f in range(STEPS):
            cols = slice(f * FB, (f + 1) * FB)
            active, slope = gelu_both(dot(normed_low, we[:, cols]))
            active = active.astype(BF)
            eg_ref[:, cols] = active
            gp_ref[:, cols] = slope.astype(BF)
            before_two = before_two + dot(active, ws[cols, :])
        b2_ref[...] = before_two
        hat = norm_parts(before_two)[0]
        mem_ref[...] = (hat * gain[1:2, :] + shift[1:2, :]).astype(BF)

    attend_unshifted()
    rest()
    in_range = jnp.logical_and(
        jnp.max(r_ref[0]) <= SHARE_MOST, jnp.min(r_ref[0]) >= 1.0 / SHARE_MOST
    )

    @pl.when(jnp.logical_not(in_range))
    def _():
        attend_shifted()
        rest()


def small_attention(q_low, k_low, v_low, bias_col):
    q_t = flip(q_low).astype(BF)
    v_t = flip(v_low).astype(BF)
    rows = head_rows(QP)
    zero = jnp.zeros_like(q_t)
    lows = []
    shares = []
    outs = []
    for pair in range(H // 2):
        wide = jnp.concatenate(
            [jnp.where(rows == 2 * pair + b, q_t, zero) for b in range(2)], axis=1
        )
        scores = dot(k_low, wide) * SCALE2 + bias_col
        exponent = jnp.exp2(scores - jnp.max(scores, axis=0, keepdims=True))
        share = 1.0 / jnp.sum(exponent, axis=0, keepdims=True)
        low = exponent.astype(BF)
        lows.append(low)
        for b in range(2):
            h = 2 * pair + b
            part = slice(b * QP, (b + 1) * QP)
            shares.append(share[:, part])
            outs.append(dot(v_t[h * HD : (h + 1) * HD, :], low[:, part]) * share[:, part])
    return lows, jnp.concatenate(shares, axis=0), jnp.concatenate(outs, axis=0)


def small_attention_back(q_low, k_low, v_low, lows, shares, o_t, grad_low):
    g_t = flip(grad_low) * spread(shares, QP)
    product = g_t * o_t
    g_t_low = g_t.astype(BF)
    g_low = g_t.T.astype(BF)
    k_t = flip(k_low).astype(BF)
    rows = head_rows(QP)
    zero = jnp.zeros_like(g_t_low)
    q_grads = []
    s_lows = []
    for pair in range(H // 2):
        wide = jnp.concatenate(
            [jnp.where(rows == 2 * pair + b, g_t_low, zero) for b in range(2)], axis=1
        )
        inner = jnp.concatenate(
            [
                jnp.sum(product[h * HD : (h + 1) * HD, :], axis=0, keepdims=True)
                for h in (2 * pair, 2 * pair + 1)
            ],
            axis=1,
        )
        s_low = (lows[pair].astype(F32) * (dot(v_low, wide) - inner)).astype(BF)
        s_lows.append(s_low)
        for b in range(2):
            h = 2 * pair + b
            q_grads.append(dot(k_t[h * HD : (h + 1) * HD, :], s_low[:, b * QP : (b + 1) * QP]))
    p_all = jnp.concatenate(lows, axis=1)
    s_all = jnp.concatenate(s_lows, axis=1)
    v_grad = dot(p_all, stacked_rows(g_low))
    k_grad = dot(s_all, stacked_rows(q_low)) * SCALE
    q_grad = jnp.concatenate(q_grads, axis=0).T * SCALE
    return q_grad, k_grad, v_grad


def decoder_kernel(
    lengths, q_ref, cot_ref, mem_ref, wp, wo, wq, wkv, wc, we, ws, gain, shift,
    keep, send, dmem_ref, out_keep, out_send, small_ref,
    units,
):
    s = section()

    def put(half, place, value):
        units[lax.rem(half + s, 2), place * D : (place + 1) * D, :] = value.astype(BF)

    def put_misc(first_unit, value):
        for c in range(value.shape[1] // D):
            half, j = divmod(first_unit + c, 4)
            put(half, 3 * j + 2, value[:, c * D : (c + 1) * D])

    t_low = q_ref[...]
    t = t_low.astype(F32)
    cot = cot_ref[...]
    self_bias = jnp.where(
        lax.broadcasted_iota(jnp.int32, (QP, 1), 0) < QUERIES, 0.0, NEGATIVE
    )
    cross_bias = jnp.where(lax.broadcasted_iota(jnp.int32, (LMAX, 1), 0) < lengths[s], 0.0, NEGATIVE)
    projected = dot(t_low, wp[...]).astype(BF)
    dq, dk, dv = projected[:, :D], projected[:, D : 2 * D], projected[:, 2 * D :]
    self_lows, self_shares, self_ot = small_attention(dq, dk, dv, self_bias)
    so = self_ot.T.astype(BF)
    hat_one, rstd_one = norm_parts(t + dot(so, wo[...]))
    d1 = hat_one * gain[0:1, :] + shift[0:1, :]
    d1_low = d1.astype(BF)
    cq = dot(d1_low, wq[...]).astype(BF)
    memory = mem_ref[...]
    pairs = dot(memory, wkv[...]).astype(BF)
    ck, cv = pairs[:, :D], pairs[:, D:]
    cross_lows, cross_shares, cross_ot = small_attention(cq, ck, cv, cross_bias)
    co = cross_ot.T.astype(BF)
    hat_two, rstd_two = norm_parts(d1 + dot(co, wc[...]))
    d2 = hat_two * gain[1:2, :] + shift[1:2, :]
    d2_low = d2.astype(BF)
    active, slope = gelu_both(dot(d2_low, we[...]))
    active = active.astype(BF)
    hat_three, rstd_three = norm_parts(d2 + dot(active, ws[...]))
    decoded = hat_three * gain[2:3, :] + shift[2:3, :]
    grad_three, gain_three, shift_three = norm_back(cot, hat_three, rstd_three, gain[2:3, :])
    branch_three = grad_three.astype(BF)
    shrink_grad = dot_tn(active, branch_three)
    for c in range(8):
        put(1, 3 * (c // 2) + c % 2, shrink_grad[c * D : (c + 1) * D, :])
    hidden_grad = (dot_nt(branch_three, ws[...]) * slope).astype(BF)
    expand_grad = dot_tn(d2_low, hidden_grad)
    for c in range(8):
        put(0, 3 * (c // 2) + c % 2, expand_grad[:, c * D : (c + 1) * D])
    grad_two, gain_two, shift_two = norm_back(
        grad_three + dot_nt(hidden_grad, we[...]), hat_two, rstd_two, gain[1:2, :]
    )
    branch_two = grad_two.astype(BF)
    put_misc(7, dot_tn(co, branch_two))
    co_grad = dot_nt(branch_two, wc[...]).astype(BF)
    cq_grad, ck_grad, cv_grad = small_attention_back(
        cq, ck, cv, cross_lows, cross_shares, cross_ot, co_grad
    )
    pairs_grad = jnp.concatenate([ck_grad, cv_grad], axis=1).astype(BF)
    dmem_ref[...] = dot_nt(pairs_grad, wkv[...]).astype(BF)
    put_misc(5, dot_tn(memory, pairs_grad))
    cq_grad = cq_grad.astype(BF)
    put_misc(4, dot_tn(d1_low, cq_grad))
    grad_one, gain_one, shift_one = norm_back(
        grad_two + dot_nt(cq_grad, wq[...]), hat_one, rstd_one, gain[0:1, :]
    )
    branch_one = grad_one.astype(BF)
    put_misc(3, dot_tn(so, branch_one))
    so_grad = dot_nt(branch_one, wo[...]).astype(BF)
    dq_grad, dk_grad, dv_grad = small_attention_back(
        dq, dk, dv, self_lows, self_shares, self_ot, so_grad
    )
    projected_grad = jnp.concatenate([dq_grad, dk_grad, dv_grad], axis=1).astype(BF)
    put_misc(0, dot_tn(t_low, projected_grad))
    queries_grad = grad_one + dot_nt(projected_grad, wp[...])
    keep[...] = units[0]
    send[...] = units[1]
    on_left = s == 0
    for n, value in enumerate((decoded, queries_grad)):
        left, right = value[:QUERIES, :LANES], value[:QUERIES, LANES:]
        out_keep[n] = jnp.where(on_left, left, right)
        out_send[n] = jnp.where(on_left, right, left)
    small_ref[...] = jnp.concatenate(
        [gain_one, gain_two, gain_three, shift_one, shift_two, shift_three, gain_one, gain_one],
        axis=0,
    )


def encoder_ff_back_kernel(
    dmem_ref, b1_ref, b2_ref, eo_ref, eg_ref, gp_ref, we, ws, wo, gain, shift, dec_small,
    keep, send, wo_grad, g1_ref, deo_ref,
    normed_low, branch, total, units, sums,
):
    j = pl.program_id(0)
    s = section()

    @pl.when(j == 0)
    def _():
        hat = norm_parts(b1_ref[...])[0]
        normed_low[...] = (hat * gain[0:1, :] + shift[0:1, :]).astype(BF)
        hat, rstd = norm_parts(b2_ref[...])
        grad_two, gain_two, shift_two = norm_back(
            dmem_ref[...].astype(F32), hat, rstd, gain[1:2, :]
        )
        total[...] = grad_two
        branch[...] = grad_two.astype(BF)
        sums[0:1, :] = gain_two
        sums[1:2, :] = shift_two

    hidden_grad = (dot_nt(branch[...], ws[...]) * gp_ref[...].astype(F32)).astype(BF)
    units[lax.rem(1 + s, 2)] = dot_tn(eg_ref[...], branch[...]).astype(BF)
    expand_grad = dot_tn(normed_low[...], hidden_grad).astype(BF)
    units[s, :D, :] = expand_grad[:, :D]
    units[s, D:, :] = expand_grad[:, D:]
    for n, ref in enumerate((keep, send)):
        ref[:, :32, :] = units[n].reshape(16, 32, D)
        ref[:, 32:, :] = jnp.zeros((16, 16, D), BF)
    total[...] += dot_nt(hidden_grad, we[...])

    @pl.when(j == STEPS - 1)
    def _():
        hat, rstd = norm_parts(b1_ref[...])
        grad_one, gain_one, shift_one = norm_back(total[...], hat, rstd, gain[0:1, :])
        g1_ref[...] = grad_one
        branch_one = grad_one.astype(BF)
        wo_grad[...] = dot_tn(eo_ref[...], branch_one).astype(BF)
        deo_ref[...] = dot_nt(branch_one, wo[...]).astype(BF)
        zero = jnp.zeros((4, D), F32)
        small = jnp.concatenate(
            [dec_small[...], gain_one, sums[0:1, :], shift_one, sums[1:2, :], zero], axis=0
        ).astype(BF)
        keep[0, 32:, :] = small
        send[0, 32:, :] = small


def attention_back_block(e_ref, eo_ref, deo_ref, p_ref, r_ref, here, kt, q_grad, k_grad, v_grad, s_all):
    values = e_ref[:, 2 * D :]
    g_t = flip(deo_ref[...]) * spread(r_ref[0], QB)
    product = g_t * flip(eo_ref[...])
    g_t_low = g_t.astype(BF)
    g_low = g_t.T.astype(BF)
    rows = head_rows(QB)
    zero = jnp.zeros_like(g_t_low)
    q_grads = []
    for h in range(H):
        inner = jnp.sum(product[h * HD : (h + 1) * HD, :], axis=0, keepdims=True)
        weights_grad = dot(values, jnp.where(rows == h, g_t_low, zero))
        p = p_ref[0, :, h * QB : (h + 1) * QB].astype(F32)
        s_low = (p * (weights_grad - inner)).astype(BF)
        s_all[:, h * QB : (h + 1) * QB] = s_low
        q_grads.append(dot(kt[h * HD : (h + 1) * HD, :], s_low))
    q_grad[...] = jnp.concatenate(q_grads, axis=0).T
    v_grad[...] += dot(p_ref[0], stacked_rows(g_low))
    k_grad[...] += dot(s_all[...], stacked_rows(e_ref[here, :D]))


def attention_back_first_kernel(
    e_ref, eo_ref, deo_ref, p_ref, r_ref,
    q_grad, k_grad, v_grad,
    kt, s_all,
):
    i = pl.program_id(0)

    @pl.when(i == 0)
    def _():
        kt[...] = flip(e_ref[:, D : 2 * D]).astype(BF)
        k_grad[...] = jnp.zeros_like(k_grad)
        v_grad[...] = jnp.zeros_like(v_grad)

    here = pl.ds(pl.multiple_of(i * QB, QB), QB)
    attention_back_block(
        e_ref, eo_ref, deo_ref, p_ref, r_ref, here, kt, q_grad, k_grad, v_grad, s_all
    )


def attention_back_last_kernel(
    e_ref, eo_ref, deo_ref, p_ref, r_ref, x_ref, g1_ref, wo_grad, wp, q_first, k_first, v_first,
    tail, img_keep, img_send,
    kt, q_grad, k_grad, v_grad, s_all,
):
    i = pl.program_id(0)
    s = section()

    @pl.when(i == 0)
    def _():
        kt[...] = flip(e_ref[:, D : 2 * D]).astype(BF)
        k_grad[...] = k_first[...]
        v_grad[...] = v_first[...]

    here = pl.ds(pl.multiple_of((i + HALF) * QB, QB), QB)
    attention_back_block(
        e_ref, eo_ref, deo_ref, p_ref, r_ref, here, kt, q_grad.at[i], k_grad, v_grad, s_all
    )

    @pl.when(i == HALF - 1)
    def _():
        q_all = jnp.concatenate([q_first[...]] + [q_grad[n] for n in range(HALF)], axis=0)
        e_grad = jnp.concatenate(
            [q_all * SCALE, k_grad[...] * SCALE, v_grad[...]], axis=1
        ).astype(BF)
        project_grad = dot_tn(x_ref[s], e_grad).astype(BF)
        for c in range(6):
            tail[c * D : (c + 1) * D, :] = project_grad[:, c * LANES : (c + 1) * LANES]
        for c in range(2):
            tail[(6 + c) * D : (7 + c) * D, :] = wo_grad[:, c * LANES : (c + 1) * LANES]
        image_grad = g1_ref[...] + dot_nt(e_grad, wp[...])
        left, right = image_grad[:, :LANES], image_grad[:, LANES:]
        on_left = s == 0
        img_keep[...] = jnp.where(on_left, left, right)
        img_send[...] = jnp.where(on_left, right, left).astype(BF)


def ordered(parts, out, section, y, x):
    for n in range(16):
        row, col = divmod(n, 4)
        from_y = lax.rem(y - row + 4, 4)
        from_x = lax.rem(x - col + 4, 4)
        last = jnp.where(section == 0, from_x, from_y)
        middle = jnp.where(section == 0, from_y, from_x)
        out[n] = parts[last, middle, 0]


def unpack_kernel(
    meta, own, other,
    project, output, query, pair, cross, dec_expand, dec_shrink, enc_expand, enc_shrink,
    dec_gain, dec_shift, enc_gain, enc_shift,
    a_ref, b_ref,
):
    j = pl.program_id(0)
    s = meta[0]
    first = s == 0
    ordered(own, a_ref, s, meta[3], meta[4])
    ordered(other, b_ref, 1 - s, meta[3], meta[4])

    def halves(start, count):
        a = a_ref[:, start : start + count, :].astype(F32).reshape(16 * count, D)
        b = b_ref[:, start : start + count, :].astype(F32).reshape(16 * count, D)
        return jnp.where(first, a, b), jnp.where(first, b, a)

    low, high = halves(0, 48)
    dec_expand[:, :D] = low[:D]
    dec_expand[:, D:] = low[D : 2 * D]
    dec_shrink[...] = high[: 2 * D]
    low_misc, high_misc = low[2 * D :], high[2 * D :]
    low, high = halves(48, 32)
    enc_expand[:, :D] = low[:D]
    enc_expand[:, D:] = low[D:]
    enc_shrink[...] = high

    @pl.when(j < 3)
    def _():
        project[...] = low_misc

    @pl.when(j == 3)
    def _():
        output[...] = low_misc
        cross[...] = high_misc
        small = a_ref[0, 80:, :].astype(F32)
        dec_gain[...] = small[0:3]
        dec_shift[...] = small[3:6]
        enc_gain[...] = small[8:10]
        enc_shift[...] = small[10:12]

    @pl.when(j == 0)
    def _():
        query[...] = high_misc

    @pl.when(jnp.logical_or(j == 1, j == 2))
    def _():
        pair[...] = high_misc


def unpack_tail_kernel(tail, project, output):
    for c in range(6):
        project[:, c * LANES : (c + 1) * LANES] = tail[c * D : (c + 1) * D, :].astype(F32)
    for c in range(2):
        output[:, c * LANES : (c + 1) * LANES] = tail[(6 + c) * D : (7 + c) * D, :].astype(F32)


def place_kernel(img_keep, img_got, dec_keep, dec_got, images, decoded, queries):
    s = section()
    on_left = s == 0
    images[s] = img_keep[...]
    images[1 - s] = img_got[...].astype(F32)
    for n, ref in enumerate((decoded, queries)):
        keep, got = dec_keep[n], dec_got[n]
        ref[:, 0, :] = jnp.where(on_left, keep, got)
        ref[:, 1, :] = jnp.where(on_left, got, keep)


def section():
    return lax.axis_index("section")


def whole(*shape):
    return pl.BlockSpec(shape, lambda i, *m: (0,) * len(shape))


def lengths_block():
    return pl.BlockSpec(memory_space=pltpu.SMEM)


def rows_block(rows, cols):
    return pl.BlockSpec((rows, cols), lambda i, *m: (i, 0))


def cols_block(rows, cols):
    return pl.BlockSpec((rows, cols), lambda i, *m: (0, i))


def call(kernel, args, in_specs, outs, scratch, steps, flops, meta=()):
    return pl.pallas_call(
        kernel,
        grid_spec=pltpu.PrefetchScalarGridSpec(
            num_scalar_prefetch=len(meta),
            grid=(steps,),
            in_specs=in_specs,
            out_specs=[spec for spec, _, _ in outs],
            scratch_shapes=[pltpu.VMEM(shape, dtype) for shape, dtype in scratch],
        ),
        out_shape=[jax.ShapeDtypeStruct(shape, dtype) for _, shape, dtype in outs],
        compiler_params=pltpu.CompilerParams(
            vmem_limit_bytes=VMEM_LIMIT, dimension_semantics=("arbitrary",)
        ),
        cost_estimate=pl.CostEstimate(flops=flops, bytes_accessed=10 * 2**20, transcendentals=0),
    )(*meta, *args)


def encoder_forward(lengths, images, wp, wo, we, ws, gain, shift):
    return call(
        encoder_forward_kernel,
        (lengths, images, wp, wo, we, ws, gain, shift),
        [lengths_block(), whole(2, LMAX, D), whole(D, 3 * D), whole(D, D), whole(D, FF), whole(FF, D), whole(2, D), whole(2, D)],
        [
            (whole(LMAX, 3 * D), (LMAX, 3 * D), BF),
            (rows_block(QB, D), (LMAX, D), BF),
            (rows_block(QB, D), (LMAX, D), F32),
            (rows_block(QB, D), (LMAX, D), F32),
            (rows_block(QB, FF), (LMAX, FF), BF),
            (rows_block(QB, FF), (LMAX, FF), BF),
            (rows_block(QB, D), (LMAX, D), BF),
            (pl.BlockSpec((1, LMAX, H * QB), lambda i: (i, 0, 0)), (STEPS, LMAX, H * QB), BF),
            (pl.BlockSpec((1, H, QB), lambda i: (i, 0, 0)), (STEPS, H, QB), F32),
        ],
        [((D, LMAX), BF), ((D, LMAX), BF), ((LMAX, 128), F32), ((D, QB), F32)],
        STEPS,
        13 * 10**9,
    )


def decoder(lengths, queries, cotangent, memory, weights):
    return call(
        decoder_kernel,
        (lengths, queries, cotangent, memory) + tuple(weights),
        [lengths_block(), whole(QP, D), whole(QP, D), whole(LMAX, D)] + [whole(*w.shape) for w in weights],
        [
            (whole(12 * D, D), (12 * D, D), BF),
            (whole(12 * D, D), (12 * D, D), BF),
            (whole(LMAX, D), (LMAX, D), BF),
            (whole(2, QUERIES, LANES), (2, QUERIES, LANES), F32),
            (whole(2, QUERIES, LANES), (2, QUERIES, LANES), F32),
            (whole(8, D), (8, D), F32),
        ],
        [((2, 12 * D, D), BF)],
        1,
        6 * 10**9,
    )


def chunk_block(rows):
    return pl.BlockSpec((16, rows, D), lambda i: (i, 0, 0))


def encoder_ff_back(dmem, b1, b2, eo, eg, gp, we, ws, wo, gain, shift, dec_small):
    return call(
        encoder_ff_back_kernel,
        (dmem, b1, b2, eo, eg, gp, we, ws, wo, gain, shift, dec_small),
        [whole(LMAX, D)] * 4
        + [cols_block(LMAX, FB), cols_block(LMAX, FB), cols_block(D, FB), rows_block(FB, D)]
        + [whole(D, D), whole(2, D), whole(2, D), whole(8, D)],
        [
            (chunk_block(48), (64, 48, D), BF),
            (chunk_block(48), (64, 48, D), BF),
            (whole(D, D), (D, D), BF),
            (whole(LMAX, D), (LMAX, D), F32),
            (whole(LMAX, D), (LMAX, D), BF),
        ],
        [((LMAX, D), BF), ((LMAX, D), BF), ((LMAX, D), F32), ((2, 2 * D, D), BF), ((8, D), F32)],
        STEPS,
        6 * 10**9,
    )


def later_rows(rows, cols):
    return pl.BlockSpec((rows, cols), lambda i: (i + HALF, 0))


def attention_back_first(e, eo, deo, p, r):
    return call(
        attention_back_first_kernel,
        (e, eo, deo, p, r),
        [
            whole(LMAX, 3 * D),
            rows_block(QB, D),
            rows_block(QB, D),
            pl.BlockSpec((1, LMAX, H * QB), lambda i: (i, 0, 0)),
            pl.BlockSpec((1, H, QB), lambda i: (i, 0, 0)),
        ],
        [
            (rows_block(QB, D), (HALF * QB, D), F32),
            (whole(LMAX, D), (LMAX, D), F32),
            (whole(LMAX, D), (LMAX, D), F32),
        ],
        [((D, LMAX), BF), ((LMAX, H * QB), BF)],
        HALF,
        13 * 10**9,
    )


def attention_back_last(e, eo, deo, p, r, images, g1, wo_grad, wp, sums):
    return call(
        attention_back_last_kernel,
        (e, eo, deo, p, r, images, g1, wo_grad, wp) + tuple(sums),
        [
            whole(LMAX, 3 * D),
            later_rows(QB, D),
            later_rows(QB, D),
            pl.BlockSpec((1, LMAX, H * QB), lambda i: (i + HALF, 0, 0)),
            pl.BlockSpec((1, H, QB), lambda i: (i + HALF, 0, 0)),
            whole(2, LMAX, D),
            whole(LMAX, D),
            whole(D, D),
            whole(D, 3 * D),
            whole(HALF * QB, D),
            whole(LMAX, D),
            whole(LMAX, D),
        ],
        [
            (whole(8 * D, LANES), (8 * D, LANES), BF),
            (whole(LMAX, LANES), (LMAX, LANES), F32),
            (whole(LMAX, LANES), (LMAX, LANES), BF),
        ],
        [((D, LMAX), BF), ((HALF, QB, D), F32), ((LMAX, D), F32), ((LMAX, D), F32), ((LMAX, H * QB), BF)],
        HALF,
        13 * 10**9,
    )


def plane_block():
    return pl.BlockSpec(
        (4, 4, 1, 96, D), lambda i, m: (0, 0, lax.rem(m[2] - i + 4, 4), 0, 0)
    )


def unpack(meta, own, other):
    return call(
        unpack_kernel,
        (own, other),
        [plane_block(), plane_block()],
        [
            (pl.BlockSpec((D, D), lambda i, m: (0, jnp.minimum(i, 2))), (D, 3 * D), F32),
            (whole(D, D), (D, D), F32),
            (whole(D, D), (D, D), F32),
            (pl.BlockSpec((D, D), lambda i, m: (0, jnp.minimum(jnp.maximum(i - 1, 0), 1))), (D, 2 * D), F32),
            (whole(D, D), (D, D), F32),
            (cols_block(D, 2 * D), (D, FF), F32),
            (rows_block(2 * D, D), (FF, D), F32),
            (cols_block(D, 2 * D), (D, FF), F32),
            (rows_block(2 * D, D), (FF, D), F32),
            (whole(3, D), (3, D), F32),
            (whole(3, D), (3, D), F32),
            (whole(2, D), (2, D), F32),
            (whole(2, D), (2, D), F32),
        ],
        [((16, 96, D), BF), ((16, 96, D), BF)],
        4,
        10**7,
        (meta,),
    )


def unpack_tail(tail):
    return call(
        unpack_tail_kernel,
        (tail,),
        [whole(8 * D, LANES)],
        [(whole(D, 3 * D), (D, 3 * D), F32), (whole(D, D), (D, D), F32)],
        [],
        1,
        10**6,
    )


def place(img_keep, img_got, dec_keep, dec_got):
    pair = (2, QUERIES, LANES)
    rows = (QUERIES, 2, LANES)
    images, decoded, queries = call(
        place_kernel,
        (img_keep, img_got, dec_keep, dec_got),
        [whole(LMAX, LANES), whole(LMAX, LANES), whole(*pair), whole(*pair)],
        [
            (whole(2, LMAX, LANES), (2, LMAX, LANES), F32),
            (whole(*rows), rows, F32),
            (whole(*rows), rows, F32),
        ],
        [],
        1,
        10**6,
    )
    return images, jnp.swapaxes(decoded, 0, 1), jnp.swapaxes(queries, 0, 1)


def swapped(a):
    return lax.ppermute(a, "section", [(0, 1), (1, 0)])


def scattered(pieces, axes):
    return lax.all_to_all(pieces, axes, 0, 0)


def summed(got):
    return jnp.sum(got.astype(F32), axis=0).astype(BF)


def spread_to(own, axes):
    count = lax.axis_size(axes)
    return lax.all_to_all(jnp.broadcast_to(own[None], (count,) + own.shape), axes, 0, 0)


STRIDES = {"x": 1, "y": 4, "z": 16}


def stage(a, axis_of_section):
    def moved(by):
        pairs = []
        for section, axis in enumerate(axis_of_section):
            stride = STRIDES[axis]
            for i in range(64):
                c = (i // stride) % 4
                to = i + ((c + by) % 4 - c) * stride
                pairs.append((section * 64 + i, section * 64 + to))
        return lax.ppermute(a, ("section", "dp"), pairs)

    one, three, two = moved(1), moved(3), moved(2)
    return jnp.stack([a, one, two, three])


def tied(*arrays):
    return lax.optimization_barrier(arrays)


def per_device(
    images,
    queries,
    lengths,
    cotangent,
    encoder_project,
    encoder_output,
    encoder_expand,
    encoder_shrink,
    encoder_gain,
    encoder_shift,
    decoder_project,
    decoder_output,
    cross_query,
    cross_keyvalue,
    cross_output,
    decoder_expand,
    decoder_shrink,
    decoder_gain,
    decoder_shift,
):
    first = section() == 0
    chips = lax.axis_size("dp")
    chip = lax.axis_index("dp")

    def padded(a):
        return jnp.pad(jnp.where(first, a[0], a[1]), ((0, QP - QUERIES), (0, 0)))

    def added(a, b):
        return (a.astype(F32) + b.astype(F32)).astype(BF).reshape(chips, -1, D)

    e, eo, b1, b2, eg, gp, memory, p, r = encoder_forward(
        lengths, images, encoder_project, encoder_output, encoder_expand, encoder_shrink,
        encoder_gain, encoder_shift,
    )
    dec_keep, dec_send, dmem, dec_mine, dec_give, dec_small = decoder(
        lengths, padded(queries), padded(cotangent), memory,
        (decoder_project, decoder_output, cross_query, cross_keyvalue, cross_output,
         decoder_expand, decoder_shrink, decoder_gain, decoder_shift),
    )
    dec_pieces = added(dec_keep, swapped(dec_send))
    dec_pieces, dmem = tied(dec_pieces, dmem)
    dec_parts = scattered(dec_pieces, "dp")
    ff_keep, ff_send, wo_grad, g1, deo = encoder_ff_back(
        dmem, b1, b2, eo, eg, gp, encoder_expand, encoder_shrink, encoder_output,
        encoder_gain, encoder_shift, dec_small,
    )
    ff_got = swapped(ff_send)
    sums = attention_back_first(e, eo, deo, p, r)
    ff_got, sums = tied(ff_got, sums)
    ff_pieces = added(ff_keep, ff_got)
    dec_parts, ff_pieces, sums = tied(dec_parts, ff_pieces, sums)
    ff_parts = scattered(ff_pieces, "dp")
    tail, img_keep, img_send = attention_back_last(
        e, eo, deo, p, r, images, g1, wo_grad, encoder_project, sums
    )
    dec_parts, ff_parts, tail = tied(dec_parts, ff_parts, tail)
    everyone = ("section", "dp")
    tail_parts = scattered(tail.reshape(2 * chips, -1, LANES), everyone)
    img_got = swapped(img_send)
    dec_got = swapped(dec_give)
    bulk = jnp.concatenate([summed(dec_parts), summed(ff_parts)])
    bulk = stage(bulk, "zz")
    bulk = stage(bulk, "yx")
    bulk, tail_parts = tied(bulk, tail_parts)
    tail = spread_to(summed(tail_parts), everyone)
    bulk = stage(bulk, "xy")
    images_out, decoded_out, queries_out = place(img_keep, img_got, dec_mine, dec_got)
    bulk, tail, images_out = tied(bulk, tail, images_out)
    project_out, output_out = unpack_tail(tail.reshape(8 * D, LANES))
    meta = jnp.stack([section(), 0, chip // 16, (chip // 4) % 4, chip % 4]).astype(jnp.int32)
    outs = unpack(meta, bulk, swapped(bulk))
    return (
        decoded_out,
        images_out,
        queries_out,
        project_out,
        output_out,
        outs[7],
        outs[8],
        outs[11],
        outs[12],
        *outs[:7],
        outs[9],
        outs[10],
    )


def solution(mesh):
    over_images = P("dp", None, None)
    split = P("dp", None, "section")
    return jax.shard_map(
        per_device,
        mesh=mesh,
        in_specs=(over_images, over_images, P("dp"), over_images) + (P(),) * 15,
        out_specs=(split,) * 3 + (P(),) * 15,
        check_vma=False,
    )
```

```python
import jax
import jax.numpy as jnp
from jax import lax
from jax.experimental import pallas as pl
from jax.experimental.pallas import tpu as pltpu
from jax.sharding import PartitionSpec as P

D = 256
H = 8
HD = 32
FF = 2048
QUERIES = 100
QP = 128
LANES = 128
LMAX = 1024
QB = 256
STEPS = LMAX // QB
HALF = STEPS // 2
FB = FF // STEPS
KT = 512
SHARE_MOST = 2.0**40

BF = jnp.bfloat16
F32 = jnp.float32
EPSILON = 1e-05
NEGATIVE = -1e30
SCALE = HD**-0.5
SCALE2 = SCALE * 1.4426950408889634
GELU_C = 0.7978845608028654
GELU_A = 0.044715
VMEM_LIMIT = 60 * 2**20


def dot(a, b):
    return lax.dot_general(a, b, (((1,), (0,)), ((), ())), preferred_element_type=F32)


def dot_nt(a, b):
    return lax.dot_general(a, b, (((1,), (1,)), ((), ())), preferred_element_type=F32)


def dot_tn(a, b):
    return lax.dot_general(a, b, (((0,), (0,)), ((), ())), preferred_element_type=F32)


def flip(a):
    return a.astype(F32).T


def norm_parts(totals):
    centered = totals - jnp.mean(totals, axis=-1, keepdims=True)
    rstd = lax.rsqrt(jnp.mean(centered * centered, axis=-1, keepdims=True) + EPSILON)
    return centered * rstd, rstd


def norm_back(grad, hat, rstd, gain_row):
    scaled = grad * gain_row
    inner = jnp.mean(scaled * hat, axis=-1, keepdims=True)
    grad_in = rstd * (scaled - jnp.mean(scaled, axis=-1, keepdims=True) - hat * inner)
    gain_grad = jnp.sum(grad * hat, axis=0, keepdims=True)
    shift_grad = jnp.sum(grad, axis=0, keepdims=True)
    return grad_in, gain_grad, shift_grad


def gelu_both(v):
    w = (GELU_C * GELU_A) * (v * v) + GELU_C
    half = 0.5 * jnp.tanh(v * w) + 0.5
    active = v * half
    slope = half + active * (1.0 - half) * (6.0 * w - 4.0 * GELU_C)
    return active, slope


def head_rows(n):
    return lax.broadcasted_iota(jnp.int32, (D, n), 0) >> 5


def head_lanes(n):
    return lax.broadcasted_iota(jnp.int32, (n, D), 1) >> 5


def stacked_rows(a):
    lanes = head_lanes(a.shape[0])
    zero = jnp.zeros_like(a)
    return jnp.concatenate([jnp.where(lanes == h, a, zero) for h in range(H)], axis=0)


def spread(rows, n):
    return jnp.concatenate(
        [jnp.broadcast_to(rows[h : h + 1, :], (HD, n)) for h in range(H)], axis=0
    )


def small_attention(q_low, k_low, v_low, bias_col):
    q_t = flip(q_low).astype(BF)
    v_t = flip(v_low).astype(BF)
    rows = head_rows(QP)
    zero = jnp.zeros_like(q_t)
    lows = []
    shares = []
    outs = []
    for pair in range(H // 2):
        wide = jnp.concatenate(
            [jnp.where(rows == 2 * pair + b, q_t, zero) for b in range(2)], axis=1
        )
        scores = dot(k_low, wide) * SCALE2 + bias_col
        exponent = jnp.exp2(scores - jnp.max(scores, axis=0, keepdims=True))
        share = 1.0 / jnp.sum(exponent, axis=0, keepdims=True)
        low = exponent.astype(BF)
        lows.append(low)
        for b in range(2):
            h = 2 * pair + b
            part = slice(b * QP, (b + 1) * QP)
            shares.append(share[:, part])
            outs.append(dot(v_t[h * HD : (h + 1) * HD, :], low[:, part]) * share[:, part])
    return lows, jnp.concatenate(shares, axis=0), jnp.concatenate(outs, axis=0)


def small_attention_back(q_low, k_low, v_low, lows, shares, o_t, grad_low):
    g_t = flip(grad_low) * spread(shares, QP)
    product = g_t * o_t
    g_t_low = g_t.astype(BF)
    g_low = g_t.T.astype(BF)
    k_t = flip(k_low).astype(BF)
    rows = head_rows(QP)
    zero = jnp.zeros_like(g_t_low)
    q_grads = []
    s_lows = []
    for pair in range(H // 2):
        wide = jnp.concatenate(
            [jnp.where(rows == 2 * pair + b, g_t_low, zero) for b in range(2)], axis=1
        )
        inner = jnp.concatenate(
            [
                jnp.sum(product[h * HD : (h + 1) * HD, :], axis=0, keepdims=True)
                for h in (2 * pair, 2 * pair + 1)
            ],
            axis=1,
        )
        s_low = (lows[pair].astype(F32) * (dot(v_low, wide) - inner)).astype(BF)
        s_lows.append(s_low)
        for b in range(2):
            h = 2 * pair + b
            q_grads.append(dot(k_t[h * HD : (h + 1) * HD, :], s_low[:, b * QP : (b + 1) * QP]))
    p_all = jnp.concatenate(lows, axis=1)
    s_all = jnp.concatenate(s_lows, axis=1)
    v_grad = dot(p_all, stacked_rows(g_low))
    k_grad = dot(s_all, stacked_rows(q_low)) * SCALE
    q_grad = jnp.concatenate(q_grads, axis=0).T * SCALE
    return q_grad, k_grad, v_grad


def decoder_part(
    s, length, q_ref, cot_ref, mem_ref, wp, wo, wq, wkv, wc, we, ws, gain, shift,
    units, dmem_ref, out_keep, out_send,
):
    def put(half, place, value):
        value = value.astype(BF)
        for row in range(0, D, 16):
            chunk, inner = divmod(place * D + row, 48)
            units[lax.rem(half + s, 2), chunk, inner : inner + 16, :] = value[row : row + 16, :]

    def put_misc(first_unit, value):
        for c in range(value.shape[1] // D):
            half, j = divmod(first_unit + c, 4)
            put(half, 3 * j + 2, value[:, c * D : (c + 1) * D])

    t_low = q_ref[...]
    t = t_low.astype(F32)
    cot = cot_ref[...]
    self_bias = jnp.where(
        lax.broadcasted_iota(jnp.int32, (QP, 1), 0) < QUERIES, 0.0, NEGATIVE
    )
    cross_bias = jnp.where(lax.broadcasted_iota(jnp.int32, (LMAX, 1), 0) < length, 0.0, NEGATIVE)
    projected = dot(t_low, wp[...]).astype(BF)
    dq, dk, dv = projected[:, :D], projected[:, D : 2 * D], projected[:, 2 * D :]
    self_lows, self_shares, self_ot = small_attention(dq, dk, dv, self_bias)
    so = self_ot.T.astype(BF)
    hat_one, rstd_one = norm_parts(t + dot(so, wo[...]))
    d1 = hat_one * gain[0:1, :] + shift[0:1, :]
    d1_low = d1.astype(BF)
    cq = dot(d1_low, wq[...]).astype(BF)
    memory = mem_ref[...]
    pairs = dot(memory, wkv[...]).astype(BF)
    ck, cv = pairs[:, :D], pairs[:, D:]
    cross_lows, cross_shares, cross_ot = small_attention(cq, ck, cv, cross_bias)
    co = cross_ot.T.astype(BF)
    hat_two, rstd_two = norm_parts(d1 + dot(co, wc[...]))
    d2 = hat_two * gain[1:2, :] + shift[1:2, :]
    d2_low = d2.astype(BF)
    active, slope = gelu_both(dot(d2_low, we[...]))
    active = active.astype(BF)
    hat_three, rstd_three = norm_parts(d2 + dot(active, ws[...]))
    decoded = hat_three * gain[2:3, :] + shift[2:3, :]
    grad_three, gain_three, shift_three = norm_back(cot, hat_three, rstd_three, gain[2:3, :])
    branch_three = grad_three.astype(BF)
    shrink_grad = dot_tn(active, branch_three)
    for c in range(8):
        put(1, 3 * (c // 2) + c % 2, shrink_grad[c * D : (c + 1) * D, :])
    hidden_grad = (dot_nt(branch_three, ws[...]) * slope).astype(BF)
    expand_grad = dot_tn(d2_low, hidden_grad)
    for c in range(8):
        put(0, 3 * (c // 2) + c % 2, expand_grad[:, c * D : (c + 1) * D])
    grad_two, gain_two, shift_two = norm_back(
        grad_three + dot_nt(hidden_grad, we[...]), hat_two, rstd_two, gain[1:2, :]
    )
    branch_two = grad_two.astype(BF)
    put_misc(7, dot_tn(co, branch_two))
    co_grad = dot_nt(branch_two, wc[...]).astype(BF)
    cq_grad, ck_grad, cv_grad = small_attention_back(
        cq, ck, cv, cross_lows, cross_shares, cross_ot, co_grad
    )
    pairs_grad = jnp.concatenate([ck_grad, cv_grad], axis=1).astype(BF)
    dmem_ref[...] = dot_nt(pairs_grad, wkv[...]).astype(BF)
    put_misc(5, dot_tn(memory, pairs_grad))
    cq_grad = cq_grad.astype(BF)
    put_misc(4, dot_tn(d1_low, cq_grad))
    grad_one, gain_one, shift_one = norm_back(
        grad_two + dot_nt(cq_grad, wq[...]), hat_one, rstd_one, gain[0:1, :]
    )
    branch_one = grad_one.astype(BF)
    put_misc(3, dot_tn(so, branch_one))
    so_grad = dot_nt(branch_one, wo[...]).astype(BF)
    dq_grad, dk_grad, dv_grad = small_attention_back(
        dq, dk, dv, self_lows, self_shares, self_ot, so_grad
    )
    projected_grad = jnp.concatenate([dq_grad, dk_grad, dv_grad], axis=1).astype(BF)
    put_misc(0, dot_tn(t_low, projected_grad))
    queries_grad = grad_one + dot_nt(projected_grad, wp[...])
    on_left = s == 0
    for n, value in enumerate((decoded, queries_grad)):
        left, right = value[:QUERIES, :LANES], value[:QUERIES, LANES:]
        out_keep[n] = jnp.where(on_left, left, right)
        out_send[n] = jnp.where(on_left, right, left)
    return jnp.concatenate(
        [gain_one, gain_two, gain_three, shift_one, shift_two, shift_three, gain_one, gain_one],
        axis=0,
    )


def main_kernel(
    lengths, q_ref, cot_ref, e_gain, e_shift, d_gain, d_shift,
    x_hbm, ewp_hbm, ewo_hbm, ewe_hbm, ews_hbm,
    dwp_hbm, dwo_hbm, dwq_hbm, dwkv_hbm, dwc_hbm, dwe_hbm, dws_hbm,
    keep, send, p_hbm, e_hbm, eo_hbm, deo_hbm, g1_hbm, r_ref, wo_grad, out_keep, out_send,
    x_ref, ewp, ewo, ewe, ews, dwp, dwo, dwq, dwkv, dwc, dwe, dws,
    e_ref, qt, vt, bias, ot, eo_ref, b1_ref, b2_ref, eg_ref, gp_ref, mem_ref, p_buf, units, dmem,
    normed_low, branch, total, deo, load_sems, p_sems, out_sems, unit_sems,
):
    s = section()
    pairs = (
        (x_hbm.at[s], x_ref), (ewp_hbm, ewp), (ewo_hbm, ewo), (ewe_hbm, ewe), (ews_hbm, ews),
        (dwp_hbm, dwp), (dwo_hbm, dwo), (dwq_hbm, dwq), (dwkv_hbm, dwkv), (dwc_hbm, dwc),
        (dwe_hbm, dwe), (dws_hbm, dws),
    )
    loads = [
        pltpu.make_async_copy(source, target, load_sems.at[n])
        for n, (source, target) in enumerate(pairs)
    ]
    for load in loads:
        load.start()
    saves = [
        pltpu.make_async_copy(source, target, out_sems.at[n])
        for n, (source, target) in enumerate(
            ((e_ref, e_hbm), (eo_ref, eo_hbm), (deo, deo_hbm), (total, g1_hbm))
        )
    ]
    rows = lax.broadcasted_iota(jnp.int32, (LMAX, 128), 0)
    bias[...] = jnp.where(rows < lengths[s], 0.0, NEGATIVE)
    units[:, :, 80:, :] = jnp.zeros((2, 64, 16, D), BF)
    loads[0].wait()
    loads[1].wait()
    e_ref[...] = dot(x_ref[...], ewp[...]).astype(BF)
    saves[0].start()
    qt[...] = flip(e_ref[:, :D]).astype(BF)
    vt[...] = flip(e_ref[:, 2 * D :]).astype(BF)

    def p_save(i, slot):
        return pltpu.make_async_copy(p_buf.at[slot], p_hbm.at[i], p_sems.at[slot])

    def forward_block(i):
        slot = lax.rem(i, 2)

        @pl.when(i >= 2)
        def _():
            p_save(i - 2, slot).wait()

        here = pl.ds(pl.multiple_of(i * QB, QB), QB)
        q_block = qt[:, here]
        rows = head_rows(QB)
        zero = jnp.zeros_like(q_block)

        def mix(h, k):
            return dot(
                vt[h * HD : (h + 1) * HD, k : k + KT],
                p_buf[slot, k : k + KT, h * QB : (h + 1) * QB],
            )

        def attend_unshifted():
            shares = [None] * H
            for h in range(H + 1):
                total_row = jnp.zeros((1, QB), F32)
                mixed = jnp.zeros((HD, QB), F32)
                for k in range(0, LMAX, KT):
                    if h < H:
                        scores = dot(
                            e_ref[k : k + KT, D : 2 * D], jnp.where(rows == h, q_block, zero)
                        )
                        scores = scores * SCALE2
                        if k + KT > LMAX // 2:
                            scores = scores + bias[k : k + KT, 0:1]
                        exponent = jnp.exp2(scores)
                        total_row = total_row + jnp.sum(exponent, axis=0, keepdims=True)
                        p_buf[slot, k : k + KT, h * QB : (h + 1) * QB] = exponent.astype(BF)
                    if h > 0:
                        mixed = mixed + mix(h - 1, k)
                if h < H:
                    shares[h] = 1.0 / total_row
                    r_ref[i, h : h + 1, :] = shares[h]
                if h > 0:
                    ot[(h - 1) * HD : h * HD, :] = mixed * shares[h - 1]

        def attend_shifted():
            for h in range(H):
                scores = dot(e_ref[:, D : 2 * D], jnp.where(rows == h, q_block, zero))
                scores = scores * SCALE2 + bias[:, 0:1]
                exponent = jnp.exp2(scores - jnp.max(scores, axis=0, keepdims=True))
                share = 1.0 / jnp.sum(exponent, axis=0, keepdims=True)
                p_buf[slot, :, h * QB : (h + 1) * QB] = exponent.astype(BF)
                r_ref[i, h : h + 1, :] = share
                ot[h * HD : (h + 1) * HD, :] = (
                    dot(vt[h * HD : (h + 1) * HD, :], exponent.astype(BF)) * share
                )

        def rest():
            attended = ot[...].T.astype(BF)
            eo_ref[here, :] = attended
            before_one = x_ref[here, :].astype(F32) + dot(attended, ewo[...])
            b1_ref[here, :] = before_one
            hat = norm_parts(before_one)[0]
            normed = hat * e_gain[0:1, :] + e_shift[0:1, :]
            low = normed.astype(BF)
            before_two = normed
            for f in range(STEPS):
                cols = slice(f * FB, (f + 1) * FB)
                active, slope = gelu_both(dot(low, ewe[:, cols]))
                active = active.astype(BF)
                eg_ref[here, cols] = active
                gp_ref[here, cols] = slope.astype(BF)
                before_two = before_two + dot(active, ews[cols, :])
            b2_ref[here, :] = before_two
            hat = norm_parts(before_two)[0]
            mem_ref[here, :] = (hat * e_gain[1:2, :] + e_shift[1:2, :]).astype(BF)

        attend_unshifted()

        @pl.when(i == 0)
        def _():
            for load in loads[2:5]:
                load.wait()

        rest()
        in_range = jnp.logical_and(
            jnp.max(r_ref[i]) <= SHARE_MOST, jnp.min(r_ref[i]) >= 1.0 / SHARE_MOST
        )

        @pl.when(jnp.logical_not(in_range))
        def _():
            attend_shifted()
            rest()

        p_save(i, slot).start()

    pl.loop(0, STEPS)(forward_block)
    saves[1].start()
    for load in loads[5:]:
        load.wait()
    dec_small = decoder_part(
        s, lengths[s], q_ref, cot_ref, mem_ref, dwp, dwo, dwq, dwkv, dwc, dwe, dws, d_gain, d_shift,
        units, dmem, out_keep, out_send,
    )

    def unit_save(n, ref, part, chunks, low, high):
        return pltpu.make_async_copy(
            units.at[n, chunks, low:high, :], ref.at[chunks, low:high, :], unit_sems.at[n, part]
        )

    unit_saves = [
        unit_save(n, ref, STEPS, slice(0, 64), 0, 48) for n, ref in enumerate((keep, send))
    ]
    for save in unit_saves:
        save.start()
    hat, rstd = norm_parts(b2_ref[...])
    grad_two, gain_two, shift_two = norm_back(dmem[...].astype(F32), hat, rstd, e_gain[1:2, :])
    total[...] = grad_two
    branch[...] = grad_two.astype(BF)
    hat, rstd = norm_parts(b1_ref[...])
    b1_ref[...] = hat
    normed_low[...] = (hat * e_gain[0:1, :] + e_shift[0:1, :]).astype(BF)
    for j in range(STEPS):
        cols = slice(j * FB, (j + 1) * FB)
        chunks = slice(16 * j, 16 * (j + 1))
        hidden_grad = dot_nt(branch[...], ews[cols, :]) * gp_ref[:, cols].astype(F32)
        hidden_grad = hidden_grad.astype(BF)
        shrink_grad = dot_tn(eg_ref[:, cols], branch[...]).astype(BF)
        units[lax.rem(1 + s, 2), chunks, 48:80, :] = shrink_grad.reshape(16, 32, D)
        expand_grad = dot_tn(normed_low[...], hidden_grad).astype(BF)
        for c in range(2):
            part = expand_grad[:, c * D : (c + 1) * D].reshape(8, 32, D)
            units[s, 16 * j + 8 * c : 16 * j + 8 * (c + 1), 48:80, :] = part
        total[...] += dot_nt(hidden_grad, ewe[:, cols])
        if j < STEPS - 1:
            for n, ref in enumerate((keep, send)):
                unit_saves.append(unit_save(n, ref, j, chunks, 48, 96))
                unit_saves[-1].start()
    grad_one, gain_one, shift_one = norm_back(total[...], b1_ref[...], rstd, e_gain[0:1, :])
    small = jnp.concatenate(
        [dec_small, gain_one, gain_two, shift_one, shift_two, jnp.zeros((4, D), F32)], axis=0
    ).astype(BF)
    for n, ref in enumerate((keep, send)):
        units[n, 48, 80:, :] = small
        unit_saves.append(unit_save(n, ref, STEPS - 1, slice(48, 64), 48, 96))
        unit_saves[-1].start()
    branch_one = grad_one.astype(BF)
    deo[...] = dot_nt(branch_one, ewo[...]).astype(BF)
    saves[2].start()
    total[...] = grad_one
    saves[3].start()
    wo_grad[...] = dot_tn(eo_ref[...], branch_one).astype(BF)
    for i in (STEPS - 2, STEPS - 1):
        p_save(i, i % 2).wait()
    for save in saves + unit_saves:
        save.wait()


def attention_back_kernel(
    e_ref, eo_ref, deo_ref, r_ref, wo_grad, p_hbm, x_hbm, g1_hbm, wp_hbm,
    tail, img_keep, img_send,
    kt, q_grad, k_grad, v_grad, s_all, p_buf, x_ref, g1_ref, wp, p_sems, sems,
):
    i = pl.program_id(0)
    s = section()
    slot = lax.rem(i, 2)
    wide = H * QB // 2

    def p_load(block, where, part):
        cols = slice(part * wide, (part + 1) * wide)
        return pltpu.make_async_copy(
            p_hbm.at[block, :, cols], p_buf.at[where, :, cols], p_sems.at[where, part]
        )

    late = [
        pltpu.make_async_copy(source, target, sems.at[n])
        for n, (source, target) in enumerate(((x_hbm.at[s], x_ref), (g1_hbm, g1_ref), (wp_hbm, wp)))
    ]

    @pl.when(i == 0)
    def _():
        for part in range(2):
            p_load(0, 0, part).start()
        for part in range(2):
            p_load(1, 1, part).start()
        for load in late:
            load.start()
        kt[...] = flip(e_ref[:, D : 2 * D]).astype(BF)
        k_grad[...] = jnp.zeros_like(k_grad)
        v_grad[...] = jnp.zeros_like(v_grad)

    @pl.when(jnp.logical_and(i > 0, i < STEPS - 1))
    def _():
        for part in range(2):
            p_load(i + 1, 1 - slot, part).start()

    g_t = flip(deo_ref[...]) * spread(r_ref[0], QB)
    product = g_t * flip(eo_ref[...])
    g_t_low = g_t.astype(BF)
    g_low = g_t.T.astype(BF)
    rows = head_rows(QB)
    zero = jnp.zeros_like(g_t_low)
    q_grads = []
    for h in range(H + 1):
        mixed = jnp.zeros((HD, QB), F32)
        if h < H:
            if h % (H // 2) == 0:
                p_load(i, slot, h // (H // 2)).wait()
            head = jnp.where(rows == h, g_t_low, zero)
            inner = jnp.sum(product[h * HD : (h + 1) * HD, :], axis=0, keepdims=True)
        for k in range(0, LMAX, KT):
            tile = slice(k, k + KT)
            if h < H:
                cols = slice(h * QB, (h + 1) * QB)
                weights_grad = dot(e_ref[tile, 2 * D :], head)
                p = p_buf[slot, tile, cols].astype(F32)
                s_all[tile, cols] = (p * (weights_grad - inner)).astype(BF)
            if h > 0:
                cols = slice((h - 1) * QB, h * QB)
                mixed = mixed + dot(kt[(h - 1) * HD : h * HD, tile], s_all[tile, cols])
        if h > 0:
            q_grads.append(mixed)
    here = pl.ds(pl.multiple_of(i * QB, QB), QB)
    q_grad[here, :] = jnp.concatenate(q_grads, axis=0).T
    v_grad[...] += dot(p_buf[slot], stacked_rows(g_low))
    k_grad[...] += dot(s_all[...], stacked_rows(e_ref[here, :D]))

    @pl.when(i == STEPS - 1)
    def _():
        for load in late:
            load.wait()
        e_grad = jnp.concatenate(
            [q_grad[...] * SCALE, k_grad[...] * SCALE, v_grad[...]], axis=1
        ).astype(BF)
        project_grad = dot_tn(x_ref[...], e_grad).astype(BF)
        for c in range(6):
            tail[c * D : (c + 1) * D, :] = project_grad[:, c * LANES : (c + 1) * LANES]
        for c in range(2):
            tail[(6 + c) * D : (7 + c) * D, :] = wo_grad[:, c * LANES : (c + 1) * LANES]
        image_grad = g1_ref[...] + dot_nt(e_grad, wp[...])
        left, right = image_grad[:, :LANES], image_grad[:, LANES:]
        on_left = s == 0
        img_keep[...] = jnp.where(on_left, left, right)
        img_send[...] = jnp.where(on_left, right, left).astype(BF)


def ordered(parts, out, section, y, x):
    for n in range(16):
        row, col = divmod(n, 4)
        from_y = lax.rem(y - row + 4, 4)
        from_x = lax.rem(x - col + 4, 4)
        last = jnp.where(section == 0, from_x, from_y)
        middle = jnp.where(section == 0, from_y, from_x)
        out[n] = parts[last, middle, 0]


def unpack_kernel(
    meta, own, other,
    project, output, query, pair, cross, dec_expand, dec_shrink, enc_expand, enc_shrink,
    dec_gain, dec_shift, enc_gain, enc_shift,
    a_ref, b_ref,
):
    j = pl.program_id(0)
    s = meta[0]
    first = s == 0
    ordered(own, a_ref, s, meta[3], meta[4])
    ordered(other, b_ref, 1 - s, meta[3], meta[4])

    def halves(start, count):
        a = a_ref[:, start : start + count, :].astype(F32).reshape(16 * count, D)
        b = b_ref[:, start : start + count, :].astype(F32).reshape(16 * count, D)
        return jnp.where(first, a, b), jnp.where(first, b, a)

    low, high = halves(0, 48)
    dec_expand[:, :D] = low[:D]
    dec_expand[:, D:] = low[D : 2 * D]
    dec_shrink[...] = high[: 2 * D]
    low_misc, high_misc = low[2 * D :], high[2 * D :]
    low, high = halves(48, 32)
    enc_expand[:, :D] = low[:D]
    enc_expand[:, D:] = low[D:]
    enc_shrink[...] = high

    @pl.when(j < 3)
    def _():
        project[...] = low_misc

    @pl.when(j == 3)
    def _():
        output[...] = low_misc
        cross[...] = high_misc
        small = a_ref[0, 80:, :].astype(F32)
        dec_gain[...] = small[0:3]
        dec_shift[...] = small[3:6]
        enc_gain[...] = small[8:10]
        enc_shift[...] = small[10:12]

    @pl.when(j == 0)
    def _():
        query[...] = high_misc

    @pl.when(jnp.logical_or(j == 1, j == 2))
    def _():
        pair[...] = high_misc


def unpack_tail_kernel(tail, project, output):
    for c in range(6):
        project[:, c * LANES : (c + 1) * LANES] = tail[c * D : (c + 1) * D, :].astype(F32)
    for c in range(2):
        output[:, c * LANES : (c + 1) * LANES] = tail[(6 + c) * D : (7 + c) * D, :].astype(F32)


def place_kernel(img_keep, img_got, dec_keep, dec_got, images, decoded, queries):
    s = section()
    on_left = s == 0
    images[s] = img_keep[...]
    images[1 - s] = img_got[...].astype(F32)
    for n, ref in enumerate((decoded, queries)):
        keep, got = dec_keep[n], dec_got[n]
        ref[:, 0, :] = jnp.where(on_left, keep, got)
        ref[:, 1, :] = jnp.where(on_left, got, keep)


def section():
    return lax.axis_index("section")


def whole(*shape):
    return pl.BlockSpec(shape, lambda i, *m: (0,) * len(shape))


def in_hbm():
    return pl.BlockSpec(memory_space=pltpu.HBM)


def lengths_block():
    return pl.BlockSpec(memory_space=pltpu.SMEM)


def rows_block(rows, cols):
    return pl.BlockSpec((rows, cols), lambda i, *m: (i, 0))


def cols_block(rows, cols):
    return pl.BlockSpec((rows, cols), lambda i, *m: (0, i))


def call(kernel, args, in_specs, outs, scratch, steps, flops, meta=(), sems=()):
    return pl.pallas_call(
        kernel,
        grid_spec=pltpu.PrefetchScalarGridSpec(
            num_scalar_prefetch=len(meta),
            grid=(steps,),
            in_specs=in_specs,
            out_specs=[spec for spec, _, _ in outs],
            scratch_shapes=[pltpu.VMEM(shape, dtype) for shape, dtype in scratch]
            + [pltpu.SemaphoreType.DMA(shape) for shape in sems],
        ),
        out_shape=[jax.ShapeDtypeStruct(shape, dtype) for _, shape, dtype in outs],
        compiler_params=pltpu.CompilerParams(
            vmem_limit_bytes=VMEM_LIMIT, dimension_semantics=("arbitrary",)
        ),
        cost_estimate=pl.CostEstimate(flops=flops, bytes_accessed=10 * 2**20, transcendentals=0),
    )(*meta, *args)


def main(lengths, queries, cotangent, norms, images, weights):
    all_rows = (LMAX, D)
    pair = (2, QUERIES, LANES)
    return call(
        main_kernel,
        (lengths, queries, cotangent) + norms + (images,) + weights,
        [lengths_block(), whole(QP, D), whole(QP, D)]
        + [whole(*a.shape) for a in norms]
        + [in_hbm()] * (1 + len(weights)),
        [
            (in_hbm(), (64, 96, D), BF),
            (in_hbm(), (64, 96, D), BF),
            (in_hbm(), (STEPS, LMAX, H * QB), BF),
            (in_hbm(), (LMAX, 3 * D), BF),
            (in_hbm(), all_rows, BF),
            (in_hbm(), all_rows, BF),
            (in_hbm(), all_rows, F32),
            (whole(STEPS, H, QB), (STEPS, H, QB), F32),
            (whole(D, D), (D, D), BF),
            (whole(*pair), pair, F32),
            (whole(*pair), pair, F32),
        ],
        [(all_rows, BF)]
        + [(a.shape, BF) for a in weights]
        + [
            ((LMAX, 3 * D), BF),
            ((D, LMAX), BF),
            ((D, LMAX), BF),
            ((LMAX, 128), F32),
            ((D, QB), F32),
            (all_rows, BF),
            (all_rows, F32),
            (all_rows, F32),
            ((LMAX, FF), BF),
            ((LMAX, FF), BF),
            (all_rows, BF),
            ((2, LMAX, H * QB), BF),
            ((2, 64, 96, D), BF),
            (all_rows, BF),
            (all_rows, BF),
            (all_rows, BF),
            (all_rows, F32),
            (all_rows, BF),
        ],
        1,
        25 * 10**9,
        sems=((12,), (2,), (4,), (2, STEPS + 1)),
    )


def attention_back(e, eo, deo, r, wo_grad, p, images, g1, wp):
    return call(
        attention_back_kernel,
        (e, eo, deo, r, wo_grad, p, images, g1, wp),
        [
            whole(LMAX, 3 * D),
            rows_block(QB, D),
            rows_block(QB, D),
            pl.BlockSpec((1, H, QB), lambda i: (i, 0, 0)),
            whole(D, D),
        ]
        + [in_hbm()] * 4,
        [
            (whole(8 * D, LANES), (8 * D, LANES), BF),
            (whole(LMAX, LANES), (LMAX, LANES), F32),
            (whole(LMAX, LANES), (LMAX, LANES), BF),
        ],
        [
            ((D, LMAX), BF),
            ((LMAX, D), F32),
            ((LMAX, D), F32),
            ((LMAX, D), F32),
            ((LMAX, H * QB), BF),
            ((2, LMAX, H * QB), BF),
            ((LMAX, D), BF),
            ((LMAX, D), F32),
            ((D, 3 * D), BF),
        ],
        STEPS,
        26 * 10**9,
        sems=((2, 2), (3,)),
    )


def plane_block():
    return pl.BlockSpec(
        (4, 4, 1, 96, D), lambda i, m: (0, 0, lax.rem(m[2] - i + 4, 4), 0, 0)
    )


def unpack(meta, own, other):
    return call(
        unpack_kernel,
        (own, other),
        [plane_block(), plane_block()],
        [
            (pl.BlockSpec((D, D), lambda i, m: (0, jnp.minimum(i, 2))), (D, 3 * D), F32),
            (whole(D, D), (D, D), F32),
            (whole(D, D), (D, D), F32),
            (pl.BlockSpec((D, D), lambda i, m: (0, jnp.minimum(jnp.maximum(i - 1, 0), 1))), (D, 2 * D), F32),
            (whole(D, D), (D, D), F32),
            (cols_block(D, 2 * D), (D, FF), F32),
            (rows_block(2 * D, D), (FF, D), F32),
            (cols_block(D, 2 * D), (D, FF), F32),
            (rows_block(2 * D, D), (FF, D), F32),
            (whole(3, D), (3, D), F32),
            (whole(3, D), (3, D), F32),
            (whole(2, D), (2, D), F32),
            (whole(2, D), (2, D), F32),
        ],
        [((16, 96, D), BF), ((16, 96, D), BF)],
        4,
        10**7,
        (meta,),
    )


def unpack_tail(tail):
    return call(
        unpack_tail_kernel,
        (tail,),
        [whole(8 * D, LANES)],
        [(whole(D, 3 * D), (D, 3 * D), F32), (whole(D, D), (D, D), F32)],
        [],
        1,
        10**6,
    )


def place(img_keep, img_got, dec_keep, dec_got):
    pair = (2, QUERIES, LANES)
    rows = (QUERIES, 2, LANES)
    images, decoded, queries = call(
        place_kernel,
        (img_keep, img_got, dec_keep, dec_got),
        [whole(LMAX, LANES), whole(LMAX, LANES), whole(*pair), whole(*pair)],
        [
            (whole(2, LMAX, LANES), (2, LMAX, LANES), F32),
            (whole(*rows), rows, F32),
            (whole(*rows), rows, F32),
        ],
        [],
        1,
        10**6,
    )
    return images, jnp.swapaxes(decoded, 0, 1), jnp.swapaxes(queries, 0, 1)


def swapped(a):
    return lax.ppermute(a, "section", [(0, 1), (1, 0)])


def scattered(pieces, axes):
    return lax.all_to_all(pieces, axes, 0, 0)


def summed(got):
    return jnp.sum(got.astype(F32), axis=0).astype(BF)


def spread_to(own, axes):
    count = lax.axis_size(axes)
    return lax.all_to_all(jnp.broadcast_to(own[None], (count,) + own.shape), axes, 0, 0)


STRIDES = {"x": 1, "y": 4, "z": 16}


def stage(a, axis_of_section):
    def moved(by):
        pairs = []
        for section, axis in enumerate(axis_of_section):
            stride = STRIDES[axis]
            for i in range(64):
                c = (i // stride) % 4
                to = i + ((c + by) % 4 - c) * stride
                pairs.append((section * 64 + i, section * 64 + to))
        return lax.ppermute(a, ("section", "dp"), pairs)

    one, three, two = moved(1), moved(3), moved(2)
    return jnp.stack([a, one, two, three])


def tied(*arrays):
    return lax.optimization_barrier(arrays)


def per_device(
    images,
    queries,
    lengths,
    cotangent,
    encoder_project,
    encoder_output,
    encoder_expand,
    encoder_shrink,
    encoder_gain,
    encoder_shift,
    decoder_project,
    decoder_output,
    cross_query,
    cross_keyvalue,
    cross_output,
    decoder_expand,
    decoder_shrink,
    decoder_gain,
    decoder_shift,
):
    first = section() == 0
    chips = lax.axis_size("dp")
    chip = lax.axis_index("dp")

    def padded(a):
        return jnp.pad(jnp.where(first, a[0], a[1]), ((0, QP - QUERIES), (0, 0)))

    def added(a, b):
        return (a.astype(F32) + b.astype(F32)).astype(BF).reshape(chips, -1, D)

    keep, send, p, e, eo, deo, g1, r, wo_grad, dec_mine, dec_give = main(
        lengths, padded(queries), padded(cotangent),
        (encoder_gain, encoder_shift, decoder_gain, decoder_shift),
        images,
        (encoder_project, encoder_output, encoder_expand, encoder_shrink,
         decoder_project, decoder_output, cross_query, cross_keyvalue, cross_output,
         decoder_expand, decoder_shrink),
    )
    pieces = added(keep, swapped(send))
    pieces, deo = tied(pieces, deo)
    parts = scattered(pieces, "dp")
    tail, img_keep, img_send = attention_back(
        e, eo, deo, r, wo_grad, p, images, g1, encoder_project
    )
    parts, tail = tied(parts, tail)
    everyone = ("section", "dp")
    tail_parts = scattered(tail.reshape(2 * chips, -1, LANES), everyone)
    img_got = swapped(img_send)
    dec_got = swapped(dec_give)
    bulk = stage(summed(parts), "zz")
    bulk = stage(bulk, "yx")
    bulk, tail_parts = tied(bulk, tail_parts)
    tail = spread_to(summed(tail_parts), everyone)
    bulk = stage(bulk, "xy")
    images_out, decoded_out, queries_out = place(img_keep, img_got, dec_mine, dec_got)
    bulk, tail, images_out = tied(bulk, tail, images_out)
    project_out, output_out = unpack_tail(tail.reshape(8 * D, LANES))
    meta = jnp.stack([section(), 0, chip // 16, (chip // 4) % 4, chip % 4]).astype(jnp.int32)
    outs = unpack(meta, bulk, swapped(bulk))
    return (
        decoded_out,
        images_out,
        queries_out,
        project_out,
        output_out,
        outs[7],
        outs[8],
        outs[11],
        outs[12],
        *outs[:7],
        outs[9],
        outs[10],
    )


def solution(mesh):
    over_images = P("dp", None, None)
    split = P("dp", None, "section")
    return jax.shard_map(
        per_device,
        mesh=mesh,
        in_specs=(over_images, over_images, P("dp"), over_images) + (P(),) * 15,
        out_specs=(split,) * 3 + (P(),) * 15,
        check_vma=False,
    )
```

```python
import jax
import jax.numpy as jnp
from jax import lax
from jax.experimental import pallas as pl
from jax.experimental.pallas import tpu as pltpu
from jax.sharding import PartitionSpec as P

D = 256
H = 8
HD = 32
FF = 2048
QUERIES = 100
QP = 128
LANES = 128
LMAX = 1024
QB = 256
STEPS = LMAX // QB
HALF = STEPS // 2
FB = FF // STEPS
KT = 512
SHARE_MOST = 2.0**40

BF = jnp.bfloat16
F32 = jnp.float32
EPSILON = 1e-05
NEGATIVE = -1e30
SCALE = HD**-0.5
SCALE2 = SCALE * 1.4426950408889634
GELU_C = 0.7978845608028654
GELU_A = 0.044715


def dot(a, b):
    return lax.dot_general(a, b, (((1,), (0,)), ((), ())), preferred_element_type=F32)


def dot_nt(a, b):
    return lax.dot_general(a, b, (((1,), (1,)), ((), ())), preferred_element_type=F32)


def dot_tn(a, b):
    return lax.dot_general(a, b, (((0,), (0,)), ((), ())), preferred_element_type=F32)


def flip(a):
    return a.astype(F32).T


def norm_parts(totals):
    centered = totals - jnp.mean(totals, axis=-1, keepdims=True)
    rstd = lax.rsqrt(jnp.mean(centered * centered, axis=-1, keepdims=True) + EPSILON)
    return centered * rstd, rstd


def norm_back(grad, hat, rstd, gain_row):
    scaled = grad * gain_row
    inner = jnp.mean(scaled * hat, axis=-1, keepdims=True)
    grad_in = rstd * (scaled - jnp.mean(scaled, axis=-1, keepdims=True) - hat * inner)
    gain_grad = jnp.sum(grad * hat, axis=0, keepdims=True)
    shift_grad = jnp.sum(grad, axis=0, keepdims=True)
    return grad_in, gain_grad, shift_grad


def gelu_both(v):
    w = (GELU_C * GELU_A) * (v * v) + GELU_C
    half = 0.5 * jnp.tanh(v * w) + 0.5
    active = v * half
    slope = half + active * (1.0 - half) * (6.0 * w - 4.0 * GELU_C)
    return active, slope


def head_rows(n):
    return lax.broadcasted_iota(jnp.int32, (D, n), 0) >> 5


def head_lanes(n):
    return lax.broadcasted_iota(jnp.int32, (n, D), 1) >> 5


def stacked_rows(a):
    lanes = head_lanes(a.shape[0])
    zero = jnp.zeros_like(a)
    return jnp.concatenate([jnp.where(lanes == h, a, zero) for h in range(H)], axis=0)


def spread(rows, n):
    return jnp.concatenate(
        [jnp.broadcast_to(rows[h : h + 1, :], (HD, n)) for h in range(H)], axis=0
    )


def small_attention(q_low, k_low, v_low, bias_col):
    q_t = flip(q_low).astype(BF)
    v_t = flip(v_low).astype(BF)
    rows = head_rows(QP)
    zero = jnp.zeros_like(q_t)
    lows = []
    shares = []
    outs = []
    for pair in range(H // 2):
        wide = jnp.concatenate(
            [jnp.where(rows == 2 * pair + b, q_t, zero) for b in range(2)], axis=1
        )
        scores = dot(k_low, wide) * SCALE2 + bias_col
        exponent = jnp.exp2(scores - jnp.max(scores, axis=0, keepdims=True))
        share = 1.0 / jnp.sum(exponent, axis=0, keepdims=True)
        low = exponent.astype(BF)
        lows.append(low)
        for b in range(2):
            h = 2 * pair + b
            part = slice(b * QP, (b + 1) * QP)
            shares.append(share[:, part])
            outs.append(dot(v_t[h * HD : (h + 1) * HD, :], low[:, part]) * share[:, part])
    return lows, jnp.concatenate(shares, axis=0), jnp.concatenate(outs, axis=0)


def small_attention_back(q_low, k_low, v_low, lows, shares, o_t, grad_low):
    g_t = flip(grad_low) * spread(shares, QP)
    product = g_t * o_t
    g_t_low = g_t.astype(BF)
    g_low = g_t.T.astype(BF)
    k_t = flip(k_low).astype(BF)
    rows = head_rows(QP)
    zero = jnp.zeros_like(g_t_low)
    q_grads = []
    s_lows = []
    for pair in range(H // 2):
        wide = jnp.concatenate(
            [jnp.where(rows == 2 * pair + b, g_t_low, zero) for b in range(2)], axis=1
        )
        inner = jnp.concatenate(
            [
                jnp.sum(product[h * HD : (h + 1) * HD, :], axis=0, keepdims=True)
                for h in (2 * pair, 2 * pair + 1)
            ],
            axis=1,
        )
        s_low = (lows[pair].astype(F32) * (dot(v_low, wide) - inner)).astype(BF)
        s_lows.append(s_low)
        for b in range(2):
            h = 2 * pair + b
            q_grads.append(dot(k_t[h * HD : (h + 1) * HD, :], s_low[:, b * QP : (b + 1) * QP]))
    p_all = jnp.concatenate(lows, axis=1)
    s_all = jnp.concatenate(s_lows, axis=1)
    v_grad = dot(p_all, stacked_rows(g_low))
    k_grad = dot(s_all, stacked_rows(q_low)) * SCALE
    q_grad = jnp.concatenate(q_grads, axis=0).T * SCALE
    return q_grad, k_grad, v_grad


def decoder_part(
    s, length, q_ref, cot_ref, mem_ref, wp, wo, wq, wkv, wc, we, ws, gain, shift,
    where, units, dmem_ref, out_keep, out_send,
):
    def put(half, place, value):
        value = value.astype(BF)
        for row in range(0, D, 16):
            chunk, inner = divmod(place * D + row, 48)
            first, second = where(half, chunk)
            units[first, second, inner : inner + 16, :] = value[row : row + 16, :]

    def put_misc(first_unit, value):
        for c in range(value.shape[1] // D):
            half, j = divmod(first_unit + c, 4)
            put(half, 3 * j + 2, value[:, c * D : (c + 1) * D])

    t_low = q_ref[...]
    t = t_low.astype(F32)
    cot = cot_ref[...]
    self_bias = jnp.where(
        lax.broadcasted_iota(jnp.int32, (QP, 1), 0) < QUERIES, 0.0, NEGATIVE
    )
    cross_bias = jnp.where(lax.broadcasted_iota(jnp.int32, (LMAX, 1), 0) < length, 0.0, NEGATIVE)
    projected = dot(t_low, wp[...]).astype(BF)
    dq, dk, dv = projected[:, :D], projected[:, D : 2 * D], projected[:, 2 * D :]
    self_lows, self_shares, self_ot = small_attention(dq, dk, dv, self_bias)
    so = self_ot.T.astype(BF)
    hat_one, rstd_one = norm_parts(t + dot(so, wo[...]))
    d1 = hat_one * gain[0:1, :] + shift[0:1, :]
    d1_low = d1.astype(BF)
    cq = dot(d1_low, wq[...]).astype(BF)
    memory = mem_ref[...]
    pairs = dot(memory, wkv[...]).astype(BF)
    ck, cv = pairs[:, :D], pairs[:, D:]
    cross_lows, cross_shares, cross_ot = small_attention(cq, ck, cv, cross_bias)
    co = cross_ot.T.astype(BF)
    hat_two, rstd_two = norm_parts(d1 + dot(co, wc[...]))
    d2 = hat_two * gain[1:2, :] + shift[1:2, :]
    d2_low = d2.astype(BF)
    active, slope = gelu_both(dot(d2_low, we[...]))
    active = active.astype(BF)
    hat_three, rstd_three = norm_parts(d2 + dot(active, ws[...]))
    decoded = hat_three * gain[2:3, :] + shift[2:3, :]
    grad_three, gain_three, shift_three = norm_back(cot, hat_three, rstd_three, gain[2:3, :])
    branch_three = grad_three.astype(BF)
    shrink_grad = dot_tn(active, branch_three)
    for c in range(8):
        put(1, 3 * (c // 2) + c % 2, shrink_grad[c * D : (c + 1) * D, :])
    hidden_grad = (dot_nt(branch_three, ws[...]) * slope).astype(BF)
    expand_grad = dot_tn(d2_low, hidden_grad)
    for c in range(8):
        put(0, 3 * (c // 2) + c % 2, expand_grad[:, c * D : (c + 1) * D])
    grad_two, gain_two, shift_two = norm_back(
        grad_three + dot_nt(hidden_grad, we[...]), hat_two, rstd_two, gain[1:2, :]
    )
    branch_two = grad_two.astype(BF)
    put_misc(7, dot_tn(co, branch_two))
    co_grad = dot_nt(branch_two, wc[...]).astype(BF)
    cq_grad, ck_grad, cv_grad = small_attention_back(
        cq, ck, cv, cross_lows, cross_shares, cross_ot, co_grad
    )
    pairs_grad = jnp.concatenate([ck_grad, cv_grad], axis=1).astype(BF)
    dmem_ref[...] = dot_nt(pairs_grad, wkv[...]).astype(BF)
    put_misc(5, dot_tn(memory, pairs_grad))
    cq_grad = cq_grad.astype(BF)
    put_misc(4, dot_tn(d1_low, cq_grad))
    grad_one, gain_one, shift_one = norm_back(
        grad_two + dot_nt(cq_grad, wq[...]), hat_one, rstd_one, gain[0:1, :]
    )
    branch_one = grad_one.astype(BF)
    put_misc(3, dot_tn(so, branch_one))
    so_grad = dot_nt(branch_one, wo[...]).astype(BF)
    dq_grad, dk_grad, dv_grad = small_attention_back(
        dq, dk, dv, self_lows, self_shares, self_ot, so_grad
    )
    projected_grad = jnp.concatenate([dq_grad, dk_grad, dv_grad], axis=1).astype(BF)
    put_misc(0, dot_tn(t_low, projected_grad))
    queries_grad = grad_one + dot_nt(projected_grad, wp[...])
    on_left = s == 0
    for n, value in enumerate((decoded, queries_grad)):
        left, right = value[:QUERIES, :LANES], value[:QUERIES, LANES:]
        out_keep[n] = jnp.where(on_left, left, right)
        out_send[n] = jnp.where(on_left, right, left)
    return jnp.concatenate(
        [gain_one, gain_two, gain_three, shift_one, shift_two, shift_three, gain_one, gain_one],
        axis=0,
    )


def coordinates():
    chip = lax.axis_index("dp")
    return chip >> 4, (chip >> 2) & 3, chip & 3


def position(half, chunk):
    z, y, x = coordinates()
    far_z = ((chunk >> 4) - z) & 3
    far_y = (((chunk >> 2) & 3) - y) & 3
    far_x = ((chunk & 3) - x) & 3
    first, second = (far_x, far_y) if half == 0 else (far_y, far_x)
    return first * 16 + second * 4 + far_z


def main_kernel(
    lengths, q_ref, cot_ref, e_gain, e_shift, d_gain, d_shift,
    x_hbm, ewp_hbm, ewo_hbm, ewe_hbm, ews_hbm,
    dwp_hbm, dwo_hbm, dwq_hbm, dwkv_hbm, dwc_hbm, dwe_hbm, dws_hbm,
    keep_0, keep_1, keep_2, keep_3, send_0, send_1, send_2, send_3, p_hbm, e_hbm, eo_hbm, deo_hbm, g1_hbm, r_ref, wo_grad, out_keep, out_send,
    x_ref, ewp, ewo, ewe, ews, dwp, dwo, dwq, dwkv, dwc, dwe, dws,
    e_ref, qt, vt, bias, ot, eo_ref, b1_ref, b2_ref, eg_ref, gp_ref, mem_ref, p_buf, units, dmem,
    normed_low, branch, total, deo, load_sems, p_sems, out_sems, unit_sems,
):
    s = section()
    pairs = (
        (x_hbm.at[s], x_ref), (ewp_hbm, ewp), (ewo_hbm, ewo), (ewe_hbm, ewe), (ews_hbm, ews),
        (dwp_hbm, dwp), (dwo_hbm, dwo), (dwq_hbm, dwq), (dwkv_hbm, dwkv), (dwc_hbm, dwc),
        (dwe_hbm, dwe), (dws_hbm, dws),
    )
    loads = [
        pltpu.make_async_copy(source, target, load_sems.at[n])
        for n, (source, target) in enumerate(pairs)
    ]
    for load in loads:
        load.start()
    saves = [
        pltpu.make_async_copy(source, target, out_sems.at[n])
        for n, (source, target) in enumerate(
            ((e_ref, e_hbm), (eo_ref, eo_hbm), (deo, deo_hbm), (total, g1_hbm))
        )
    ]
    rows = lax.broadcasted_iota(jnp.int32, (LMAX, 128), 0)
    bias[...] = jnp.where(rows < lengths[s], 0.0, NEGATIVE)
    units[:, :, 80:, :] = jnp.zeros((2, 64, 16, D), BF)
    loads[0].wait()
    loads[1].wait()
    e_ref[...] = dot(x_ref[...], ewp[...]).astype(BF)
    saves[0].start()
    qt[...] = flip(e_ref[:, :D]).astype(BF)
    vt[...] = flip(e_ref[:, 2 * D :]).astype(BF)

    def p_save(i, slot):
        return pltpu.make_async_copy(p_buf.at[slot], p_hbm.at[i], p_sems.at[slot])

    def forward_block(i, shifted):
        slot = lax.rem(i, 2)

        @pl.when(i >= 2)
        def _():
            p_save(i - 2, slot).wait()

        here = pl.ds(pl.multiple_of(i * QB, QB), QB)
        q_block = qt[:, here]
        rows = head_rows(QB)
        zero = jnp.zeros_like(q_block)

        def mix(h, k):
            return dot(
                vt[h * HD : (h + 1) * HD, k : k + KT],
                p_buf[slot, k : k + KT, h * QB : (h + 1) * QB],
            )

        def attend_unshifted():
            shares = [None] * H
            for h in range(H + 1):
                total_row = jnp.zeros((1, QB), F32)
                mixed = jnp.zeros((HD, QB), F32)
                for k in range(0, LMAX, KT):
                    if h < H:
                        scores = dot(
                            e_ref[k : k + KT, D : 2 * D], jnp.where(rows == h, q_block, zero)
                        )
                        scores = scores * SCALE2
                        if k + KT > LMAX // 2:
                            scores = scores + bias[k : k + KT, 0:1]
                        exponent = jnp.exp2(scores)
                        total_row = total_row + jnp.sum(exponent, axis=0, keepdims=True)
                        p_buf[slot, k : k + KT, h * QB : (h + 1) * QB] = exponent.astype(BF)
                    if h > 0:
                        mixed = mixed + mix(h - 1, k)
                if h < H:
                    shares[h] = 1.0 / total_row
                    r_ref[i, h : h + 1, :] = shares[h]
                if h > 0:
                    ot[(h - 1) * HD : h * HD, :] = mixed * shares[h - 1]

        def attend_shifted():
            for h in range(H):
                scores = dot(e_ref[:, D : 2 * D], jnp.where(rows == h, q_block, zero))
                scores = scores * SCALE2 + bias[:, 0:1]
                exponent = jnp.exp2(scores - jnp.max(scores, axis=0, keepdims=True))
                share = 1.0 / jnp.sum(exponent, axis=0, keepdims=True)
                p_buf[slot, :, h * QB : (h + 1) * QB] = exponent.astype(BF)
                r_ref[i, h : h + 1, :] = share
                ot[h * HD : (h + 1) * HD, :] = (
                    dot(vt[h * HD : (h + 1) * HD, :], exponent.astype(BF)) * share
                )

        def rest():
            attended = ot[...].T.astype(BF)
            eo_ref[here, :] = attended
            before_one = x_ref[here, :].astype(F32) + dot(attended, ewo[...])
            b1_ref[here, :] = before_one
            hat = norm_parts(before_one)[0]
            normed = hat * e_gain[0:1, :] + e_shift[0:1, :]
            low = normed.astype(BF)
            before_two = normed
            for f in range(STEPS):
                cols = slice(f * FB, (f + 1) * FB)
                active, slope = gelu_both(dot(low, ewe[:, cols]))
                active = active.astype(BF)
                eg_ref[here, cols] = active
                gp_ref[here, cols] = slope.astype(BF)
                before_two = before_two + dot(active, ews[cols, :])
            b2_ref[here, :] = before_two
            hat = norm_parts(before_two)[0]
            mem_ref[here, :] = (hat * e_gain[1:2, :] + e_shift[1:2, :]).astype(BF)

        if shifted:
            attend_shifted()
        else:
            attend_unshifted()

            @pl.when(i == 0)
            def _():
                for load in loads[2:5]:
                    load.wait()

        rest()
        p_save(i, slot).start()

    pl.loop(0, STEPS)(lambda i: forward_block(i, False))
    in_range = jnp.logical_and(
        jnp.max(r_ref[...]) <= SHARE_MOST, jnp.min(r_ref[...]) >= 1.0 / SHARE_MOST
    )

    @pl.when(jnp.logical_not(in_range))
    def _():
        for i in (STEPS - 2, STEPS - 1):
            p_save(i, i % 2).wait()
        pl.loop(0, STEPS)(lambda i: forward_block(i, True))

    saves[1].start()
    for load in loads[5:]:
        load.wait()
    dec_small = decoder_part(
        s, lengths[s], q_ref, cot_ref, mem_ref, dwp, dwo, dwq, dwkv, dwc, dwe, dws, d_gain, d_shift,
        lambda half, chunk: (lax.rem(half + s, 2), position(half, chunk)),
        units, dmem, out_keep, out_send,
    )

    def save_units(part, low, high):
        for n, refs in enumerate(
            ((keep_0, keep_1, keep_2, keep_3), (send_0, send_1, send_2, send_3))
        ):
            for k, ref in enumerate(refs):
                save = pltpu.make_async_copy(
                    units.at[n, 16 * k : 16 * (k + 1), low:high, :],
                    ref.at[:, low:high, :],
                    unit_sems.at[n, k, part],
                )
                save.start()
                unit_saves.append(save)

    unit_saves = []
    save_units(0, 0, 48)
    hat, rstd = norm_parts(b2_ref[...])
    grad_two, gain_two, shift_two = norm_back(dmem[...].astype(F32), hat, rstd, e_gain[1:2, :])
    total[...] = grad_two
    branch[...] = grad_two.astype(BF)
    hat, rstd = norm_parts(b1_ref[...])
    b1_ref[...] = hat
    normed_low[...] = (hat * e_gain[0:1, :] + e_shift[0:1, :]).astype(BF)
    for j in range(STEPS):
        cols = slice(j * FB, (j + 1) * FB)
        hidden_grad = dot_nt(branch[...], ews[cols, :]) * gp_ref[:, cols].astype(F32)
        hidden_grad = hidden_grad.astype(BF)
        shrink_grad = dot_tn(eg_ref[:, cols], branch[...]).astype(BF)
        expand_grad = dot_tn(normed_low[...], hidden_grad).astype(BF)
        for c in range(16):
            row = 32 * (c % 8)
            part = expand_grad[row : row + 32, (c // 8) * D : (c // 8 + 1) * D]
            units[s, position(0, 16 * j + c), 48:80, :] = part
            part = shrink_grad[32 * c : 32 * (c + 1), :]
            units[lax.rem(1 + s, 2), position(1, 16 * j + c), 48:80, :] = part
        total[...] += dot_nt(hidden_grad, ewe[:, cols])
    save_units(1, 48, 80)
    grad_one, gain_one, shift_one = norm_back(total[...], b1_ref[...], rstd, e_gain[0:1, :])
    small = jnp.concatenate(
        [dec_small, gain_one, gain_two, shift_one, shift_two, jnp.zeros((4, D), F32)], axis=0
    ).astype(BF)
    for half in range(2):
        units[lax.rem(half + s, 2), position(half, 48), 80:, :] = small
    save_units(2, 80, 96)
    branch_one = grad_one.astype(BF)
    deo[...] = dot_nt(branch_one, ewo[...]).astype(BF)
    saves[2].start()
    total[...] = grad_one
    saves[3].start()
    wo_grad[...] = dot_tn(eo_ref[...], branch_one).astype(BF)
    for i in (STEPS - 2, STEPS - 1):
        p_save(i, i % 2).wait()
    for save in saves + unit_saves:
        save.wait()


def attention_back_kernel(
    e_ref, eo_ref, deo_ref, r_ref, wo_grad, p_hbm, x_hbm, g1_hbm, wp_hbm,
    tail, img_keep, img_send,
    kt, q_grad, k_grad, v_grad, s_all, p_buf, x_ref, g1_ref, wp, p_sems, sems,
):
    i = pl.program_id(0)
    s = section()
    slot = lax.rem(i, 2)
    wide = H * QB // 2

    def p_load(block, where, part):
        cols = slice(part * wide, (part + 1) * wide)
        return pltpu.make_async_copy(
            p_hbm.at[block, :, cols], p_buf.at[where, :, cols], p_sems.at[where, part]
        )

    late = [
        pltpu.make_async_copy(source, target, sems.at[n])
        for n, (source, target) in enumerate(((x_hbm.at[s], x_ref), (g1_hbm, g1_ref), (wp_hbm, wp)))
    ]

    @pl.when(i == 0)
    def _():
        for part in range(2):
            p_load(0, 0, part).start()
        for part in range(2):
            p_load(1, 1, part).start()
        for load in late:
            load.start()
        kt[...] = flip(e_ref[:, D : 2 * D]).astype(BF)
        k_grad[...] = jnp.zeros_like(k_grad)
        v_grad[...] = jnp.zeros_like(v_grad)

    @pl.when(jnp.logical_and(i > 0, i < STEPS - 1))
    def _():
        for part in range(2):
            p_load(i + 1, 1 - slot, part).start()

    g_t = flip(deo_ref[...]) * spread(r_ref[0], QB)
    product = g_t * flip(eo_ref[...])
    g_t_low = g_t.astype(BF)
    g_low = g_t.T.astype(BF)
    rows = head_rows(QB)
    zero = jnp.zeros_like(g_t_low)
    q_grads = []
    for h in range(H + 1):
        mixed = jnp.zeros((HD, QB), F32)
        if h < H:
            if h % (H // 2) == 0:
                p_load(i, slot, h // (H // 2)).wait()
            head = jnp.where(rows == h, g_t_low, zero)
            inner = jnp.sum(product[h * HD : (h + 1) * HD, :], axis=0, keepdims=True)
        for k in range(0, LMAX, KT):
            tile = slice(k, k + KT)
            if h < H:
                cols = slice(h * QB, (h + 1) * QB)
                weights_grad = dot(e_ref[tile, 2 * D :], head)
                p = p_buf[slot, tile, cols].astype(F32)
                s_all[tile, cols] = (p * (weights_grad - inner)).astype(BF)
            if h > 0:
                cols = slice((h - 1) * QB, h * QB)
                mixed = mixed + dot(kt[(h - 1) * HD : h * HD, tile], s_all[tile, cols])
        if h > 0:
            q_grads.append(mixed)
    here = pl.ds(pl.multiple_of(i * QB, QB), QB)
    q_grad[here, :] = jnp.concatenate(q_grads, axis=0).T
    v_grad[...] += dot(p_buf[slot], stacked_rows(g_low))
    k_grad[...] += dot(s_all[...], stacked_rows(e_ref[here, :D]))

    @pl.when(i == STEPS - 1)
    def _():
        for load in late:
            load.wait()
        e_grad = jnp.concatenate(
            [q_grad[...] * SCALE, k_grad[...] * SCALE, v_grad[...]], axis=1
        ).astype(BF)
        project_grad = dot_tn(x_ref[...], e_grad).astype(BF)
        for c in range(6):
            tail[c * D : (c + 1) * D, :] = project_grad[:, c * LANES : (c + 1) * LANES]
        for c in range(2):
            tail[(6 + c) * D : (7 + c) * D, :] = wo_grad[:, c * LANES : (c + 1) * LANES]
        image_grad = g1_ref[...] + dot_nt(e_grad, wp[...])
        left, right = image_grad[:, :LANES], image_grad[:, LANES:]
        on_left = s == 0
        img_keep[...] = jnp.where(on_left, left, right)
        img_send[...] = jnp.where(on_left, right, left).astype(BF)


def ordered(pieces, out, half, y, x):
    on_x = half == 0
    for k, piece in enumerate(pieces):
        for m in range(4):
            row = jnp.where(on_x, y - m, y - k) & 3
            col = jnp.where(on_x, x - k, x - m) & 3
            out[row * 4 + col] = piece[m, 0]


def unpack_kernel(
    meta, own_0, own_1, own_2, own_3, other_0, other_1, other_2, other_3,
    project, output, query, pair, cross, dec_expand, dec_shrink, enc_expand, enc_shrink,
    dec_gain, dec_shift, enc_gain, enc_shift,
    a_ref, b_ref,
):
    j = pl.program_id(0)
    s = section()
    first = s == 0
    _, y, x = coordinates()
    ordered((own_0, own_1, own_2, own_3), a_ref, s, y, x)
    ordered((other_0, other_1, other_2, other_3), b_ref, 1 - s, y, x)

    def halves(start, count):
        a = a_ref[:, start : start + count, :].astype(F32).reshape(16 * count, D)
        b = b_ref[:, start : start + count, :].astype(F32).reshape(16 * count, D)
        return jnp.where(first, a, b), jnp.where(first, b, a)

    low, high = halves(0, 48)
    dec_expand[:, :D] = low[:D]
    dec_expand[:, D:] = low[D : 2 * D]
    dec_shrink[...] = high[: 2 * D]
    low_misc, high_misc = low[2 * D :], high[2 * D :]
    low, high = halves(48, 32)
    enc_expand[:, :D] = low[:D]
    enc_expand[:, D:] = low[D:]
    enc_shrink[...] = high

    @pl.when(j < 3)
    def _():
        project[...] = low_misc

    @pl.when(j == 3)
    def _():
        output[...] = low_misc
        cross[...] = high_misc
        small = a_ref[0, 80:, :].astype(F32)
        dec_gain[...] = small[0:3]
        dec_shift[...] = small[3:6]
        enc_gain[...] = small[8:10]
        enc_shift[...] = small[10:12]

    @pl.when(j == 0)
    def _():
        query[...] = high_misc

    @pl.when(jnp.logical_or(j == 1, j == 2))
    def _():
        pair[...] = high_misc


def unpack_tail_kernel(tail, project, output):
    for c in range(6):
        project[:, c * LANES : (c + 1) * LANES] = tail[c * D : (c + 1) * D, :].astype(F32)
    for c in range(2):
        output[:, c * LANES : (c + 1) * LANES] = tail[(6 + c) * D : (7 + c) * D, :].astype(F32)


def place_kernel(img_keep, img_got, dec_keep, dec_got, images, decoded, queries):
    s = section()
    on_left = s == 0
    images[s] = img_keep[...]
    images[1 - s] = img_got[...].astype(F32)
    for n, ref in enumerate((decoded, queries)):
        keep, got = dec_keep[n], dec_got[n]
        ref[:, 0, :] = jnp.where(on_left, keep, got)
        ref[:, 1, :] = jnp.where(on_left, got, keep)


def section():
    return lax.axis_index("section")


def whole(*shape):
    return pl.BlockSpec(shape, lambda i, *m: (0,) * len(shape))


def in_hbm():
    return pl.BlockSpec(memory_space=pltpu.HBM)


def lengths_block():
    return pl.BlockSpec(memory_space=pltpu.SMEM)


def rows_block(rows, cols):
    return pl.BlockSpec((rows, cols), lambda i, *m: (i, 0))


def cols_block(rows, cols):
    return pl.BlockSpec((rows, cols), lambda i, *m: (0, i))


def call(kernel, args, in_specs, outs, scratch, steps, flops, meta=(), sems=(), vmem=60):
    return pl.pallas_call(
        kernel,
        grid_spec=pltpu.PrefetchScalarGridSpec(
            num_scalar_prefetch=len(meta),
            grid=(steps,),
            in_specs=in_specs,
            out_specs=[spec for spec, _, _ in outs],
            scratch_shapes=[pltpu.VMEM(shape, dtype) for shape, dtype in scratch]
            + [pltpu.SemaphoreType.DMA(shape) for shape in sems],
        ),
        out_shape=[jax.ShapeDtypeStruct(shape, dtype) for _, shape, dtype in outs],
        compiler_params=pltpu.CompilerParams(
            vmem_limit_bytes=vmem * 2**20, dimension_semantics=("arbitrary",)
        ),
        cost_estimate=pl.CostEstimate(flops=flops, bytes_accessed=10 * 2**20, transcendentals=0),
    )(*meta, *args)


def main(lengths, queries, cotangent, norms, images, weights):
    all_rows = (LMAX, D)
    pair = (2, QUERIES, LANES)
    return call(
        main_kernel,
        (lengths, queries, cotangent) + norms + (images,) + weights,
        [lengths_block(), whole(QP, D), whole(QP, D)]
        + [whole(*a.shape) for a in norms]
        + [in_hbm()] * (1 + len(weights)),
        [
            *[(in_hbm(), (16, 96, D), BF)] * 8,
            (in_hbm(), (STEPS, LMAX, H * QB), BF),
            (in_hbm(), (LMAX, 3 * D), BF),
            (in_hbm(), all_rows, BF),
            (in_hbm(), all_rows, BF),
            (in_hbm(), all_rows, F32),
            (whole(STEPS, H, QB), (STEPS, H, QB), F32),
            (whole(D, D), (D, D), BF),
            (whole(*pair), pair, F32),
            (whole(*pair), pair, F32),
        ],
        [(all_rows, BF)]
        + [(a.shape, BF) for a in weights]
        + [
            ((LMAX, 3 * D), BF),
            ((D, LMAX), BF),
            ((D, LMAX), BF),
            ((LMAX, 128), F32),
            ((D, QB), F32),
            (all_rows, BF),
            (all_rows, F32),
            (all_rows, F32),
            ((LMAX, FF), BF),
            ((LMAX, FF), BF),
            (all_rows, BF),
            ((2, LMAX, H * QB), BF),
            ((2, 64, 96, D), BF),
            (all_rows, BF),
            (all_rows, BF),
            (all_rows, BF),
            (all_rows, F32),
            (all_rows, BF),
        ],
        1,
        25 * 10**9,
        sems=((12,), (2,), (4,), (2, 4, 3)),
    )


def attention_back(e, eo, deo, r, wo_grad, p, images, g1, wp):
    return call(
        attention_back_kernel,
        (e, eo, deo, r, wo_grad, p, images, g1, wp),
        [
            whole(LMAX, 3 * D),
            rows_block(QB, D),
            rows_block(QB, D),
            pl.BlockSpec((1, H, QB), lambda i: (i, 0, 0)),
            whole(D, D),
        ]
        + [in_hbm()] * 4,
        [
            (whole(8 * D, LANES), (8 * D, LANES), BF),
            (whole(LMAX, LANES), (LMAX, LANES), F32),
            (whole(LMAX, LANES), (LMAX, LANES), BF),
        ],
        [
            ((D, LMAX), BF),
            ((LMAX, D), F32),
            ((LMAX, D), F32),
            ((LMAX, D), F32),
            ((LMAX, H * QB), BF),
            ((2, LMAX, H * QB), BF),
            ((LMAX, D), BF),
            ((LMAX, D), F32),
            ((D, 3 * D), BF),
        ],
        STEPS,
        26 * 10**9,
        sems=((2, 2), (3,)),
    )


def plane_block():
    return pl.BlockSpec(
        (4, 1, 96, D), lambda i, z: (0, lax.rem(z[0] - i + 4, 4), 0, 0)
    )


def unpack(z, own, other):
    return call(
        unpack_kernel,
        (*own, *other),
        [plane_block()] * 8,
        [
            (pl.BlockSpec((D, D), lambda i, m: (0, jnp.minimum(i, 2))), (D, 3 * D), F32),
            (whole(D, D), (D, D), F32),
            (whole(D, D), (D, D), F32),
            (pl.BlockSpec((D, D), lambda i, m: (0, jnp.minimum(jnp.maximum(i - 1, 0), 1))), (D, 2 * D), F32),
            (whole(D, D), (D, D), F32),
            (cols_block(D, 2 * D), (D, FF), F32),
            (rows_block(2 * D, D), (FF, D), F32),
            (cols_block(D, 2 * D), (D, FF), F32),
            (rows_block(2 * D, D), (FF, D), F32),
            (whole(3, D), (3, D), F32),
            (whole(3, D), (3, D), F32),
            (whole(2, D), (2, D), F32),
            (whole(2, D), (2, D), F32),
        ],
        [((16, 96, D), BF), ((16, 96, D), BF)],
        4,
        10**7,
        (z,),
        vmem=24,
    )


def unpack_tail(tail):
    return call(
        unpack_tail_kernel,
        (tail,),
        [whole(8 * D, LANES)],
        [(whole(D, 3 * D), (D, 3 * D), F32), (whole(D, D), (D, D), F32)],
        [],
        1,
        10**6,
        vmem=12,
    )


def place(img_keep, img_got, dec_keep, dec_got):
    pair = (2, QUERIES, LANES)
    rows = (QUERIES, 2, LANES)
    images, decoded, queries = call(
        place_kernel,
        (img_keep, img_got, dec_keep, dec_got),
        [whole(LMAX, LANES), whole(LMAX, LANES), whole(*pair), whole(*pair)],
        [
            (whole(2, LMAX, LANES), (2, LMAX, LANES), F32),
            (whole(*rows), rows, F32),
            (whole(*rows), rows, F32),
        ],
        [],
        1,
        10**6,
        vmem=12,
    )
    return images, jnp.swapaxes(decoded, 0, 1), jnp.swapaxes(queries, 0, 1)


def swapped(a):
    return lax.ppermute(a, "section", [(0, 1), (1, 0)])


def scattered(pieces, axes):
    return lax.all_to_all(pieces, axes, 0, 0)


def summed(got):
    return jnp.sum(got.astype(F32), axis=0).astype(BF)


def spread_to(own, axes):
    count = lax.axis_size(axes)
    return lax.all_to_all(jnp.broadcast_to(own[None], (count,) + own.shape), axes, 0, 0)


STRIDES = {"x": 1, "y": 4, "z": 16}


def moved(a, by, axis_of_section):
    pairs = []
    for index, axis in enumerate(axis_of_section):
        stride = STRIDES[axis]
        for i in range(64):
            c = (i // stride) % 4
            to = i + ((c + by) % 4 - c) * stride
            pairs.append((index * 64 + i, index * 64 + to))
    return lax.ppermute(a, ("section", "dp"), pairs)


def stage(a, axis_of_section):
    one, three, two = [moved(a, by, axis_of_section) for by in (1, 3, 2)]
    return a, one, two, three


def total_of(arrays):
    return sum(a.astype(F32) for a in arrays).astype(BF)


def reduce_stage(pieces, axis_of_section):
    one, three, two = [moved(pieces[by], by, axis_of_section) for by in (1, 3, 2)]
    return total_of((pieces[0], one, two, three))


def tied(*arrays):
    return lax.optimization_barrier(arrays)


def per_device(
    images,
    queries,
    lengths,
    cotangent,
    encoder_project,
    encoder_output,
    encoder_expand,
    encoder_shrink,
    encoder_gain,
    encoder_shift,
    decoder_project,
    decoder_output,
    cross_query,
    cross_keyvalue,
    cross_output,
    decoder_expand,
    decoder_shrink,
    decoder_gain,
    decoder_shift,
):
    first = section() == 0
    chips = lax.axis_size("dp")
    chip = lax.axis_index("dp")

    def padded(a):
        return jnp.pad(jnp.where(first, a[0], a[1]), ((0, QP - QUERIES), (0, 0)))

    def added(a, b):
        return (a.astype(F32) + b.astype(F32)).astype(BF)

    *quarters, p, e, eo, deo, g1, r, wo_grad, dec_mine, dec_give = main(
        lengths, padded(queries), padded(cotangent),
        (encoder_gain, encoder_shift, decoder_gain, decoder_shift),
        images,
        (encoder_project, encoder_output, encoder_expand, encoder_shrink,
         decoder_project, decoder_output, cross_query, cross_keyvalue, cross_output,
         decoder_expand, decoder_shrink),
    )
    order = (2, 1, 3, 0)
    got = {k: swapped(quarters[4 + k]) for k in order}
    pieces = {k: added(quarters[k], got[k]) for k in order}
    pieces[1], pieces[2], pieces[3], deo = tied(pieces[1], pieces[2], pieces[3], deo)
    received = [moved(pieces[k], k, "xy") for k in order[:3]]
    tail, img_keep, img_send = attention_back(
        e, eo, deo, r, wo_grad, p, images, g1, encoder_project
    )
    *received, tail = tied(*received, tail)
    everyone = ("section", "dp")
    tail_parts = scattered(tail.reshape(2 * chips, -1, LANES), everyone)
    img_got = swapped(img_send)
    dec_got = swapped(dec_give)
    bulk = total_of([pieces[0]] + received).reshape(4, 4, 96, D)
    bulk = reduce_stage([bulk[k] for k in range(4)], "yx")
    bulk = reduce_stage([bulk[k] for k in range(4)], "zz")
    bulk = jnp.stack(stage(bulk, "zz"))
    bulk = jnp.stack(stage(bulk, "yx"))
    bulk, tail_parts = tied(bulk, tail_parts)
    tail = spread_to(summed(tail_parts), everyone)
    own = list(stage(bulk, "xy"))
    images_out, decoded_out, queries_out = place(img_keep, img_got, dec_mine, dec_got)
    own[2], tail, images_out = tied(own[2], tail, images_out)
    project_out, output_out = unpack_tail(tail.reshape(8 * D, LANES))
    outs = unpack((chip // 16).reshape(1), own, [swapped(a) for a in own])
    return (
        decoded_out,
        images_out,
        queries_out,
        project_out,
        output_out,
        outs[7],
        outs[8],
        outs[11],
        outs[12],
        *outs[:7],
        outs[9],
        outs[10],
    )


def solution(mesh):
    over_images = P("dp", None, None)
    split = P("dp", None, "section")
    return jax.shard_map(
        per_device,
        mesh=mesh,
        in_specs=(over_images, over_images, P("dp"), over_images) + (P(),) * 15,
        out_specs=(split,) * 3 + (P(),) * 15,
        check_vma=False,
    )
```

```python
import jax
import jax.numpy as jnp
from jax import lax
from jax.experimental import pallas as pl
from jax.experimental.pallas import tpu as pltpu
from jax.sharding import PartitionSpec as P

D = 256
H = 8
HD = 32
FF = 2048
QUERIES = 100
QP = 128
LANES = 128
LMAX = 1024
QB = 256
STEPS = LMAX // QB
HALF = STEPS // 2
FB = FF // STEPS
KT = 512
SHARE_MOST = 2.0**40

BF = jnp.bfloat16
F32 = jnp.float32
EPSILON = 1e-05
NEGATIVE = -1e30
SCALE = HD**-0.5
SCALE2 = SCALE * 1.4426950408889634
GELU_C = 0.7978845608028654
GELU_A = 0.044715


def dot(a, b):
    return lax.dot_general(a, b, (((1,), (0,)), ((), ())), preferred_element_type=F32)


def dot_nt(a, b):
    return lax.dot_general(a, b, (((1,), (1,)), ((), ())), preferred_element_type=F32)


def dot_tn(a, b):
    return lax.dot_general(a, b, (((0,), (0,)), ((), ())), preferred_element_type=F32)


def flip(a):
    return a.astype(F32).T


def norm_parts(totals):
    centered = totals - jnp.mean(totals, axis=-1, keepdims=True)
    rstd = lax.rsqrt(jnp.mean(centered * centered, axis=-1, keepdims=True) + EPSILON)
    return centered * rstd, rstd


def norm_back(grad, hat, rstd, gain_row):
    scaled = grad * gain_row
    inner = jnp.mean(scaled * hat, axis=-1, keepdims=True)
    grad_in = rstd * (scaled - jnp.mean(scaled, axis=-1, keepdims=True) - hat * inner)
    gain_grad = jnp.sum(grad * hat, axis=0, keepdims=True)
    shift_grad = jnp.sum(grad, axis=0, keepdims=True)
    return grad_in, gain_grad, shift_grad


def gelu_both(v):
    w = (GELU_C * GELU_A) * (v * v) + GELU_C
    half = 0.5 * jnp.tanh(v * w) + 0.5
    active = v * half
    slope = half + active * (1.0 - half) * (6.0 * w - 4.0 * GELU_C)
    return active, slope


def head_rows(n):
    return lax.broadcasted_iota(jnp.int32, (D, n), 0) >> 5


def head_lanes(n):
    return lax.broadcasted_iota(jnp.int32, (n, D), 1) >> 5


def stacked_rows(a):
    lanes = head_lanes(a.shape[0])
    zero = jnp.zeros_like(a)
    return jnp.concatenate([jnp.where(lanes == h, a, zero) for h in range(H)], axis=0)


def spread(rows, n):
    return jnp.concatenate(
        [jnp.broadcast_to(rows[h : h + 1, :], (HD, n)) for h in range(H)], axis=0
    )


def small_attention(q_low, k_low, v_low, bias_col):
    q_t = flip(q_low).astype(BF)
    v_t = flip(v_low).astype(BF)
    rows = head_rows(QP)
    zero = jnp.zeros_like(q_t)
    lows = []
    shares = []
    outs = []
    for pair in range(H // 2):
        wide = jnp.concatenate(
            [jnp.where(rows == 2 * pair + b, q_t, zero) for b in range(2)], axis=1
        )
        scores = dot(k_low, wide) * SCALE2 + bias_col
        exponent = jnp.exp2(scores - jnp.max(scores, axis=0, keepdims=True))
        share = 1.0 / jnp.sum(exponent, axis=0, keepdims=True)
        low = exponent.astype(BF)
        lows.append(low)
        for b in range(2):
            h = 2 * pair + b
            part = slice(b * QP, (b + 1) * QP)
            shares.append(share[:, part])
            outs.append(dot(v_t[h * HD : (h + 1) * HD, :], low[:, part]) * share[:, part])
    return lows, jnp.concatenate(shares, axis=0), jnp.concatenate(outs, axis=0)


def small_attention_back(q_low, k_low, v_low, lows, shares, o_t, grad_low):
    g_t = flip(grad_low) * spread(shares, QP)
    product = g_t * o_t
    g_t_low = g_t.astype(BF)
    g_low = g_t.T.astype(BF)
    k_t = flip(k_low).astype(BF)
    rows = head_rows(QP)
    zero = jnp.zeros_like(g_t_low)
    q_grads = []
    s_lows = []
    for pair in range(H // 2):
        wide = jnp.concatenate(
            [jnp.where(rows == 2 * pair + b, g_t_low, zero) for b in range(2)], axis=1
        )
        inner = jnp.concatenate(
            [
                jnp.sum(product[h * HD : (h + 1) * HD, :], axis=0, keepdims=True)
                for h in (2 * pair, 2 * pair + 1)
            ],
            axis=1,
        )
        s_low = (lows[pair].astype(F32) * (dot(v_low, wide) - inner)).astype(BF)
        s_lows.append(s_low)
        for b in range(2):
            h = 2 * pair + b
            q_grads.append(dot(k_t[h * HD : (h + 1) * HD, :], s_low[:, b * QP : (b + 1) * QP]))
    p_all = jnp.concatenate(lows, axis=1)
    s_all = jnp.concatenate(s_lows, axis=1)
    v_grad = dot(p_all, stacked_rows(g_low))
    k_grad = dot(s_all, stacked_rows(q_low)) * SCALE
    q_grad = jnp.concatenate(q_grads, axis=0).T * SCALE
    return q_grad, k_grad, v_grad


def decoder_part(
    s, length, q_ref, cot_ref, mem_ref, wp, wo, wq, wkv, wc, we, ws, gain, shift,
    where, units, dmem_ref, out_keep, out_send,
):
    def put(half, place, value):
        value = value.astype(BF)
        for row in range(0, D, 16):
            chunk, inner = divmod(place * D + row, 48)
            first, second = where(half, chunk)
            units[first, second, inner : inner + 16, :] = value[row : row + 16, :]

    def put_misc(first_unit, value):
        for c in range(value.shape[1] // D):
            half, j = divmod(first_unit + c, 4)
            put(half, 3 * j + 2, value[:, c * D : (c + 1) * D])

    t_low = q_ref[...]
    t = t_low.astype(F32)
    cot = cot_ref[...]
    self_bias = jnp.where(
        lax.broadcasted_iota(jnp.int32, (QP, 1), 0) < QUERIES, 0.0, NEGATIVE
    )
    cross_bias = jnp.where(lax.broadcasted_iota(jnp.int32, (LMAX, 1), 0) < length, 0.0, NEGATIVE)
    projected = dot(t_low, wp[...]).astype(BF)
    dq, dk, dv = projected[:, :D], projected[:, D : 2 * D], projected[:, 2 * D :]
    self_lows, self_shares, self_ot = small_attention(dq, dk, dv, self_bias)
    so = self_ot.T.astype(BF)
    hat_one, rstd_one = norm_parts(t + dot(so, wo[...]))
    d1 = hat_one * gain[0:1, :] + shift[0:1, :]
    d1_low = d1.astype(BF)
    cq = dot(d1_low, wq[...]).astype(BF)
    memory = mem_ref[...]
    pairs = dot(memory, wkv[...]).astype(BF)
    ck, cv = pairs[:, :D], pairs[:, D:]
    cross_lows, cross_shares, cross_ot = small_attention(cq, ck, cv, cross_bias)
    co = cross_ot.T.astype(BF)
    hat_two, rstd_two = norm_parts(d1 + dot(co, wc[...]))
    d2 = hat_two * gain[1:2, :] + shift[1:2, :]
    d2_low = d2.astype(BF)
    active, slope = gelu_both(dot(d2_low, we[...]))
    active = active.astype(BF)
    hat_three, rstd_three = norm_parts(d2 + dot(active, ws[...]))
    decoded = hat_three * gain[2:3, :] + shift[2:3, :]
    grad_three, gain_three, shift_three = norm_back(cot, hat_three, rstd_three, gain[2:3, :])
    branch_three = grad_three.astype(BF)
    shrink_grad = dot_tn(active, branch_three)
    for c in range(8):
        put(1, 3 * (c // 2) + c % 2, shrink_grad[c * D : (c + 1) * D, :])
    hidden_grad = (dot_nt(branch_three, ws[...]) * slope).astype(BF)
    expand_grad = dot_tn(d2_low, hidden_grad)
    for c in range(8):
        put(0, 3 * (c // 2) + c % 2, expand_grad[:, c * D : (c + 1) * D])
    grad_two, gain_two, shift_two = norm_back(
        grad_three + dot_nt(hidden_grad, we[...]), hat_two, rstd_two, gain[1:2, :]
    )
    branch_two = grad_two.astype(BF)
    put_misc(7, dot_tn(co, branch_two))
    co_grad = dot_nt(branch_two, wc[...]).astype(BF)
    cq_grad, ck_grad, cv_grad = small_attention_back(
        cq, ck, cv, cross_lows, cross_shares, cross_ot, co_grad
    )
    pairs_grad = jnp.concatenate([ck_grad, cv_grad], axis=1).astype(BF)
    dmem_ref[...] = dot_nt(pairs_grad, wkv[...]).astype(BF)
    put_misc(5, dot_tn(memory, pairs_grad))
    cq_grad = cq_grad.astype(BF)
    put_misc(4, dot_tn(d1_low, cq_grad))
    grad_one, gain_one, shift_one = norm_back(
        grad_two + dot_nt(cq_grad, wq[...]), hat_one, rstd_one, gain[0:1, :]
    )
    branch_one = grad_one.astype(BF)
    put_misc(3, dot_tn(so, branch_one))
    so_grad = dot_nt(branch_one, wo[...]).astype(BF)
    dq_grad, dk_grad, dv_grad = small_attention_back(
        dq, dk, dv, self_lows, self_shares, self_ot, so_grad
    )
    projected_grad = jnp.concatenate([dq_grad, dk_grad, dv_grad], axis=1).astype(BF)
    put_misc(0, dot_tn(t_low, projected_grad))
    queries_grad = grad_one + dot_nt(projected_grad, wp[...])
    on_left = s == 0
    for n, value in enumerate((decoded, queries_grad)):
        left, right = value[:QUERIES, :LANES], value[:QUERIES, LANES:]
        out_keep[n] = jnp.where(on_left, left, right)
        out_send[n] = jnp.where(on_left, right, left)
    return jnp.concatenate(
        [gain_one, gain_two, gain_three, shift_one, shift_two, shift_three, gain_one, gain_one],
        axis=0,
    )


def coordinates():
    chip = lax.axis_index("dp")
    return chip >> 4, (chip >> 2) & 3, chip & 3


def position(half, chunk):
    z, y, x = coordinates()
    far_z = ((chunk >> 4) - z) & 3
    far_y = (((chunk >> 2) & 3) - y) & 3
    far_x = ((chunk & 3) - x) & 3
    first, second = (far_x, far_y) if half == 0 else (far_y, far_x)
    return first * 16 + second * 4 + far_z


def main_kernel(
    lengths, q_ref, cot_ref, e_gain, e_shift, d_gain, d_shift,
    x_hbm, ewp_hbm, ewo_hbm, ewe_hbm, ews_hbm,
    dwp_hbm, dwo_hbm, dwq_hbm, dwkv_hbm, dwc_hbm, dwe_hbm, dws_hbm,
    keep, send, p_hbm, e_hbm, eo_hbm, deo_hbm, g1_hbm, r_ref, wo_grad, out_keep, out_send,
    x_ref, ewp, ewo, ewe, ews, dwp, dwo, dwq, dwkv, dwc, dwe, dws,
    e_ref, qt, vt, bias, ot, eo_ref, b1_ref, b2_ref, eg_ref, gp_ref, mem_ref, p_buf, units, dmem,
    normed_low, branch, total, deo, load_sems, p_sems, out_sems, unit_sems,
):
    s = section()
    pairs = (
        (x_hbm.at[s], x_ref), (ewp_hbm, ewp), (ewo_hbm, ewo), (ewe_hbm, ewe), (ews_hbm, ews),
        (dwp_hbm, dwp), (dwo_hbm, dwo), (dwq_hbm, dwq), (dwkv_hbm, dwkv), (dwc_hbm, dwc),
        (dwe_hbm, dwe), (dws_hbm, dws),
    )
    loads = [
        pltpu.make_async_copy(source, target, load_sems.at[n])
        for n, (source, target) in enumerate(pairs)
    ]
    for load in loads:
        load.start()
    saves = [
        pltpu.make_async_copy(source, target, out_sems.at[n])
        for n, (source, target) in enumerate(
            ((e_ref, e_hbm), (eo_ref, eo_hbm), (deo, deo_hbm), (total, g1_hbm))
        )
    ]
    rows = lax.broadcasted_iota(jnp.int32, (LMAX, 128), 0)
    bias[...] = jnp.where(rows < lengths[s], 0.0, NEGATIVE)
    units[:, :, 80:, :] = jnp.zeros((2, 64, 16, D), BF)
    loads[0].wait()
    loads[1].wait()
    e_ref[...] = dot(x_ref[...], ewp[...]).astype(BF)
    saves[0].start()
    qt[...] = flip(e_ref[:, :D]).astype(BF)
    vt[...] = flip(e_ref[:, 2 * D :]).astype(BF)

    def p_save(i, slot):
        return pltpu.make_async_copy(p_buf.at[slot], p_hbm.at[i], p_sems.at[slot])

    def forward_block(i, shifted):
        slot = lax.rem(i, 2)

        @pl.when(i >= 2)
        def _():
            p_save(i - 2, slot).wait()

        here = pl.ds(pl.multiple_of(i * QB, QB), QB)
        q_block = qt[:, here]
        rows = head_rows(QB)
        zero = jnp.zeros_like(q_block)

        def mix(h, k):
            return dot(
                vt[h * HD : (h + 1) * HD, k : k + KT],
                p_buf[slot, k : k + KT, h * QB : (h + 1) * QB],
            )

        def attend_unshifted():
            shares = [None] * H
            for h in range(H + 1):
                total_row = jnp.zeros((1, QB), F32)
                mixed = jnp.zeros((HD, QB), F32)
                for k in range(0, LMAX, KT):
                    if h < H:
                        scores = dot(
                            e_ref[k : k + KT, D : 2 * D], jnp.where(rows == h, q_block, zero)
                        )
                        scores = scores * SCALE2
                        if k + KT > LMAX // 2:
                            scores = scores + bias[k : k + KT, 0:1]
                        exponent = jnp.exp2(scores)
                        total_row = total_row + jnp.sum(exponent, axis=0, keepdims=True)
                        p_buf[slot, k : k + KT, h * QB : (h + 1) * QB] = exponent.astype(BF)
                    if h > 0:
                        mixed = mixed + mix(h - 1, k)
                if h < H:
                    shares[h] = 1.0 / total_row
                    r_ref[i, h : h + 1, :] = shares[h]
                if h > 0:
                    ot[(h - 1) * HD : h * HD, :] = mixed * shares[h - 1]

        def attend_shifted():
            for h in range(H):
                scores = dot(e_ref[:, D : 2 * D], jnp.where(rows == h, q_block, zero))
                scores = scores * SCALE2 + bias[:, 0:1]
                exponent = jnp.exp2(scores - jnp.max(scores, axis=0, keepdims=True))
                share = 1.0 / jnp.sum(exponent, axis=0, keepdims=True)
                p_buf[slot, :, h * QB : (h + 1) * QB] = exponent.astype(BF)
                r_ref[i, h : h + 1, :] = share
                ot[h * HD : (h + 1) * HD, :] = (
                    dot(vt[h * HD : (h + 1) * HD, :], exponent.astype(BF)) * share
                )

        def rest():
            attended = ot[...].T.astype(BF)
            eo_ref[here, :] = attended
            before_one = x_ref[here, :].astype(F32) + dot(attended, ewo[...])
            b1_ref[here, :] = before_one
            hat = norm_parts(before_one)[0]
            normed = hat * e_gain[0:1, :] + e_shift[0:1, :]
            low = normed.astype(BF)
            before_two = normed
            for f in range(STEPS):
                cols = slice(f * FB, (f + 1) * FB)
                active, slope = gelu_both(dot(low, ewe[:, cols]))
                active = active.astype(BF)
                eg_ref[here, cols] = active
                gp_ref[here, cols] = slope.astype(BF)
                before_two = before_two + dot(active, ews[cols, :])
            b2_ref[here, :] = before_two
            hat = norm_parts(before_two)[0]
            mem_ref[here, :] = (hat * e_gain[1:2, :] + e_shift[1:2, :]).astype(BF)

        if shifted:
            attend_shifted()
        else:
            attend_unshifted()

            @pl.when(i == 0)
            def _():
                for load in loads[2:5]:
                    load.wait()

        rest()
        p_save(i, slot).start()

    pl.loop(0, STEPS)(lambda i: forward_block(i, False))
    in_range = jnp.logical_and(
        jnp.max(r_ref[...]) <= SHARE_MOST, jnp.min(r_ref[...]) >= 1.0 / SHARE_MOST
    )

    @pl.when(jnp.logical_not(in_range))
    def _():
        for i in (STEPS - 2, STEPS - 1):
            p_save(i, i % 2).wait()
        pl.loop(0, STEPS)(lambda i: forward_block(i, True))

    saves[1].start()
    for load in loads[5:]:
        load.wait()
    dec_small = decoder_part(
        s, lengths[s], q_ref, cot_ref, mem_ref, dwp, dwo, dwq, dwkv, dwc, dwe, dws, d_gain, d_shift,
        lambda half, chunk: (lax.rem(half + s, 2), position(half, chunk)),
        units, dmem, out_keep, out_send,
    )

    def save_units(part, low, high):
        for n, ref in enumerate((keep, send)):
            save = pltpu.make_async_copy(
                units.at[n, :, low:high, :], ref.at[:, low:high, :], unit_sems.at[n, part]
            )
            save.start()
            unit_saves.append(save)

    unit_saves = []
    save_units(0, 0, 48)
    hat, rstd = norm_parts(b2_ref[...])
    grad_two, gain_two, shift_two = norm_back(dmem[...].astype(F32), hat, rstd, e_gain[1:2, :])
    total[...] = grad_two
    branch[...] = grad_two.astype(BF)
    hat, rstd = norm_parts(b1_ref[...])
    b1_ref[...] = hat
    normed_low[...] = (hat * e_gain[0:1, :] + e_shift[0:1, :]).astype(BF)
    for j in range(STEPS):
        cols = slice(j * FB, (j + 1) * FB)
        hidden_grad = dot_nt(branch[...], ews[cols, :]) * gp_ref[:, cols].astype(F32)
        hidden_grad = hidden_grad.astype(BF)
        shrink_grad = dot_tn(eg_ref[:, cols], branch[...]).astype(BF)
        expand_grad = dot_tn(normed_low[...], hidden_grad).astype(BF)
        for c in range(16):
            row = 32 * (c % 8)
            part = expand_grad[row : row + 32, (c // 8) * D : (c // 8 + 1) * D]
            units[s, position(0, 16 * j + c), 48:80, :] = part
            part = shrink_grad[32 * c : 32 * (c + 1), :]
            units[lax.rem(1 + s, 2), position(1, 16 * j + c), 48:80, :] = part
        total[...] += dot_nt(hidden_grad, ewe[:, cols])
    save_units(1, 48, 80)
    grad_one, gain_one, shift_one = norm_back(total[...], b1_ref[...], rstd, e_gain[0:1, :])
    small = jnp.concatenate(
        [dec_small, gain_one, gain_two, shift_one, shift_two, jnp.zeros((4, D), F32)], axis=0
    ).astype(BF)
    for half in range(2):
        units[lax.rem(half + s, 2), position(half, 48), 80:, :] = small
    save_units(2, 80, 96)
    branch_one = grad_one.astype(BF)
    deo[...] = dot_nt(branch_one, ewo[...]).astype(BF)
    saves[2].start()
    total[...] = grad_one
    saves[3].start()
    wo_grad[...] = dot_tn(eo_ref[...], branch_one).astype(BF)
    for i in (STEPS - 2, STEPS - 1):
        p_save(i, i % 2).wait()
    for save in saves + unit_saves:
        save.wait()


def attention_back_kernel(
    e_ref, eo_ref, deo_ref, r_ref, wo_grad, p_hbm, x_hbm, g1_hbm, wp_hbm,
    tail, img_keep, img_send,
    kt, q_grad, k_grad, v_grad, s_all, p_buf, x_ref, g1_ref, wp, p_sems, sems,
):
    i = pl.program_id(0)
    s = section()
    slot = lax.rem(i, 2)
    wide = H * QB // 2

    def p_load(block, where, part):
        cols = slice(part * wide, (part + 1) * wide)
        return pltpu.make_async_copy(
            p_hbm.at[block, :, cols], p_buf.at[where, :, cols], p_sems.at[where, part]
        )

    late = [
        pltpu.make_async_copy(source, target, sems.at[n])
        for n, (source, target) in enumerate(((x_hbm.at[s], x_ref), (g1_hbm, g1_ref), (wp_hbm, wp)))
    ]

    @pl.when(i == 0)
    def _():
        for part in range(2):
            p_load(0, 0, part).start()
        for part in range(2):
            p_load(1, 1, part).start()
        for load in late:
            load.start()
        kt[...] = flip(e_ref[:, D : 2 * D]).astype(BF)
        k_grad[...] = jnp.zeros_like(k_grad)
        v_grad[...] = jnp.zeros_like(v_grad)

    @pl.when(jnp.logical_and(i > 0, i < STEPS - 1))
    def _():
        for part in range(2):
            p_load(i + 1, 1 - slot, part).start()

    g_t = flip(deo_ref[...]) * spread(r_ref[0], QB)
    product = g_t * flip(eo_ref[...])
    g_t_low = g_t.astype(BF)
    g_low = g_t.T.astype(BF)
    rows = head_rows(QB)
    zero = jnp.zeros_like(g_t_low)
    q_grads = []
    for h in range(H + 1):
        mixed = jnp.zeros((HD, QB), F32)
        if h < H:
            if h % (H // 2) == 0:
                p_load(i, slot, h // (H // 2)).wait()
            head = jnp.where(rows == h, g_t_low, zero)
            inner = jnp.sum(product[h * HD : (h + 1) * HD, :], axis=0, keepdims=True)
        for k in range(0, LMAX, KT):
            tile = slice(k, k + KT)
            if h < H:
                cols = slice(h * QB, (h + 1) * QB)
                weights_grad = dot(e_ref[tile, 2 * D :], head)
                p = p_buf[slot, tile, cols].astype(F32)
                s_all[tile, cols] = (p * (weights_grad - inner)).astype(BF)
            if h > 0:
                cols = slice((h - 1) * QB, h * QB)
                mixed = mixed + dot(kt[(h - 1) * HD : h * HD, tile], s_all[tile, cols])
        if h > 0:
            q_grads.append(mixed)
    here = pl.ds(pl.multiple_of(i * QB, QB), QB)
    q_grad[here, :] = jnp.concatenate(q_grads, axis=0).T
    v_grad[...] += dot(p_buf[slot], stacked_rows(g_low))
    k_grad[...] += dot(s_all[...], stacked_rows(e_ref[here, :D]))

    @pl.when(i == STEPS - 1)
    def _():
        for load in late:
            load.wait()
        e_grad = jnp.concatenate(
            [q_grad[...] * SCALE, k_grad[...] * SCALE, v_grad[...]], axis=1
        ).astype(BF)
        project_grad = dot_tn(x_ref[...], e_grad).astype(BF)
        for c in range(6):
            tail[c * D : (c + 1) * D, :] = project_grad[:, c * LANES : (c + 1) * LANES]
        for c in range(2):
            tail[(6 + c) * D : (7 + c) * D, :] = wo_grad[:, c * LANES : (c + 1) * LANES]
        image_grad = g1_ref[...] + dot_nt(e_grad, wp[...])
        left, right = image_grad[:, :LANES], image_grad[:, LANES:]
        on_left = s == 0
        img_keep[...] = jnp.where(on_left, left, right)
        img_send[...] = jnp.where(on_left, right, left).astype(BF)


def ordered(pieces, out, half, y, x):
    on_x = half == 0
    for k, piece in enumerate(pieces):
        for m in range(4):
            row = jnp.where(on_x, y - m, y - k) & 3
            col = jnp.where(on_x, x - k, x - m) & 3
            out[row * 4 + col] = piece[m, 0]


def unpack_kernel(
    meta, own_0, own_1, own_2, own_3, other_0, other_1, other_2, other_3,
    project, output, query, pair, cross, dec_expand, dec_shrink, enc_expand, enc_shrink,
    dec_gain, dec_shift, enc_gain, enc_shift,
    a_ref, b_ref,
):
    j = pl.program_id(0)
    s = section()
    first = s == 0
    _, y, x = coordinates()
    ordered((own_0, own_1, own_2, own_3), a_ref, s, y, x)
    ordered((other_0, other_1, other_2, other_3), b_ref, 1 - s, y, x)

    def halves(start, count):
        a = a_ref[:, start : start + count, :].astype(F32).reshape(16 * count, D)
        b = b_ref[:, start : start + count, :].astype(F32).reshape(16 * count, D)
        return jnp.where(first, a, b), jnp.where(first, b, a)

    low, high = halves(0, 48)
    dec_expand[:, :D] = low[:D]
    dec_expand[:, D:] = low[D : 2 * D]
    dec_shrink[...] = high[: 2 * D]
    low_misc, high_misc = low[2 * D :], high[2 * D :]
    low, high = halves(48, 32)
    enc_expand[:, :D] = low[:D]
    enc_expand[:, D:] = low[D:]
    enc_shrink[...] = high

    @pl.when(j < 3)
    def _():
        project[...] = low_misc

    @pl.when(j == 3)
    def _():
        output[...] = low_misc
        cross[...] = high_misc
        small = a_ref[0, 80:, :].astype(F32)
        dec_gain[...] = small[0:3]
        dec_shift[...] = small[3:6]
        enc_gain[...] = small[8:10]
        enc_shift[...] = small[10:12]

    @pl.when(j == 0)
    def _():
        query[...] = high_misc

    @pl.when(jnp.logical_or(j == 1, j == 2))
    def _():
        pair[...] = high_misc


def unpack_tail_kernel(tail, project, output):
    for c in range(6):
        project[:, c * LANES : (c + 1) * LANES] = tail[c * D : (c + 1) * D, :].astype(F32)
    for c in range(2):
        output[:, c * LANES : (c + 1) * LANES] = tail[(6 + c) * D : (7 + c) * D, :].astype(F32)


def place_kernel(img_keep, img_got, dec_keep, dec_got, images, decoded, queries):
    s = section()
    on_left = s == 0
    images[s] = img_keep[...]
    images[1 - s] = img_got[...].astype(F32)
    for n, ref in enumerate((decoded, queries)):
        keep, got = dec_keep[n], dec_got[n]
        ref[:, 0, :] = jnp.where(on_left, keep, got)
        ref[:, 1, :] = jnp.where(on_left, got, keep)


def section():
    return lax.axis_index("section")


def whole(*shape):
    return pl.BlockSpec(shape, lambda i, *m: (0,) * len(shape))


def in_hbm():
    return pl.BlockSpec(memory_space=pltpu.HBM)


def lengths_block():
    return pl.BlockSpec(memory_space=pltpu.SMEM)


def rows_block(rows, cols):
    return pl.BlockSpec((rows, cols), lambda i, *m: (i, 0))


def cols_block(rows, cols):
    return pl.BlockSpec((rows, cols), lambda i, *m: (0, i))


def call(kernel, args, in_specs, outs, scratch, steps, flops, meta=(), sems=(), vmem=60):
    return pl.pallas_call(
        kernel,
        grid_spec=pltpu.PrefetchScalarGridSpec(
            num_scalar_prefetch=len(meta),
            grid=(steps,),
            in_specs=in_specs,
            out_specs=[spec for spec, _, _ in outs],
            scratch_shapes=[pltpu.VMEM(shape, dtype) for shape, dtype in scratch]
            + [pltpu.SemaphoreType.DMA(shape) for shape in sems],
        ),
        out_shape=[jax.ShapeDtypeStruct(shape, dtype) for _, shape, dtype in outs],
        compiler_params=pltpu.CompilerParams(
            vmem_limit_bytes=vmem * 2**20, dimension_semantics=("arbitrary",)
        ),
        cost_estimate=pl.CostEstimate(flops=flops, bytes_accessed=10 * 2**20, transcendentals=0),
    )(*meta, *args)


def main(lengths, queries, cotangent, norms, images, weights):
    all_rows = (LMAX, D)
    pair = (2, QUERIES, LANES)
    return call(
        main_kernel,
        (lengths, queries, cotangent) + norms + (images,) + weights,
        [lengths_block(), whole(QP, D), whole(QP, D)]
        + [whole(*a.shape) for a in norms]
        + [in_hbm()] * (1 + len(weights)),
        [
            (in_hbm(), (64, 96, D), BF),
            (in_hbm(), (64, 96, D), BF),
            (in_hbm(), (STEPS, LMAX, H * QB), BF),
            (in_hbm(), (LMAX, 3 * D), BF),
            (in_hbm(), all_rows, BF),
            (in_hbm(), all_rows, BF),
            (in_hbm(), all_rows, F32),
            (whole(STEPS, H, QB), (STEPS, H, QB), F32),
            (whole(D, D), (D, D), BF),
            (whole(*pair), pair, F32),
            (whole(*pair), pair, F32),
        ],
        [(all_rows, BF)]
        + [(a.shape, BF) for a in weights]
        + [
            ((LMAX, 3 * D), BF),
            ((D, LMAX), BF),
            ((D, LMAX), BF),
            ((LMAX, 128), F32),
            ((D, QB), F32),
            (all_rows, BF),
            (all_rows, F32),
            (all_rows, F32),
            ((LMAX, FF), BF),
            ((LMAX, FF), BF),
            (all_rows, BF),
            ((2, LMAX, H * QB), BF),
            ((2, 64, 96, D), BF),
            (all_rows, BF),
            (all_rows, BF),
            (all_rows, BF),
            (all_rows, F32),
            (all_rows, BF),
        ],
        1,
        25 * 10**9,
        sems=((12,), (2,), (4,), (2, 3)),
    )


def attention_back(e, eo, deo, r, wo_grad, p, images, g1, wp):
    return call(
        attention_back_kernel,
        (e, eo, deo, r, wo_grad, p, images, g1, wp),
        [
            whole(LMAX, 3 * D),
            rows_block(QB, D),
            rows_block(QB, D),
            pl.BlockSpec((1, H, QB), lambda i: (i, 0, 0)),
            whole(D, D),
        ]
        + [in_hbm()] * 4,
        [
            (whole(8 * D, LANES), (8 * D, LANES), BF),
            (whole(LMAX, LANES), (LMAX, LANES), F32),
            (whole(LMAX, LANES), (LMAX, LANES), BF),
        ],
        [
            ((D, LMAX), BF),
            ((LMAX, D), F32),
            ((LMAX, D), F32),
            ((LMAX, D), F32),
            ((LMAX, H * QB), BF),
            ((2, LMAX, H * QB), BF),
            ((LMAX, D), BF),
            ((LMAX, D), F32),
            ((D, 3 * D), BF),
        ],
        STEPS,
        26 * 10**9,
        sems=((2, 2), (3,)),
    )


def plane_block():
    return pl.BlockSpec(
        (4, 1, 96, D), lambda i, z: (0, lax.rem(z[0] - i + 4, 4), 0, 0)
    )


def unpack(z, own, other):
    return call(
        unpack_kernel,
        (*own, *other),
        [plane_block()] * 8,
        [
            (pl.BlockSpec((D, D), lambda i, m: (0, jnp.minimum(i, 2))), (D, 3 * D), F32),
            (whole(D, D), (D, D), F32),
            (whole(D, D), (D, D), F32),
            (pl.BlockSpec((D, D), lambda i, m: (0, jnp.minimum(jnp.maximum(i - 1, 0), 1))), (D, 2 * D), F32),
            (whole(D, D), (D, D), F32),
            (cols_block(D, 2 * D), (D, FF), F32),
            (rows_block(2 * D, D), (FF, D), F32),
            (cols_block(D, 2 * D), (D, FF), F32),
            (rows_block(2 * D, D), (FF, D), F32),
            (whole(3, D), (3, D), F32),
            (whole(3, D), (3, D), F32),
            (whole(2, D), (2, D), F32),
            (whole(2, D), (2, D), F32),
        ],
        [((16, 96, D), BF), ((16, 96, D), BF)],
        4,
        10**7,
        (z,),
        vmem=24,
    )


def unpack_tail(tail):
    return call(
        unpack_tail_kernel,
        (tail,),
        [whole(8 * D, LANES)],
        [(whole(D, 3 * D), (D, 3 * D), F32), (whole(D, D), (D, D), F32)],
        [],
        1,
        10**6,
        vmem=12,
    )


def place(img_keep, img_got, dec_keep, dec_got):
    pair = (2, QUERIES, LANES)
    rows = (QUERIES, 2, LANES)
    images, decoded, queries = call(
        place_kernel,
        (img_keep, img_got, dec_keep, dec_got),
        [whole(LMAX, LANES), whole(LMAX, LANES), whole(*pair), whole(*pair)],
        [
            (whole(2, LMAX, LANES), (2, LMAX, LANES), F32),
            (whole(*rows), rows, F32),
            (whole(*rows), rows, F32),
        ],
        [],
        1,
        10**6,
        vmem=12,
    )
    return images, jnp.swapaxes(decoded, 0, 1), jnp.swapaxes(queries, 0, 1)


def swapped(a):
    return lax.ppermute(a, "section", [(0, 1), (1, 0)])


def scattered(pieces, axes):
    return lax.all_to_all(pieces, axes, 0, 0)


def summed(got):
    return jnp.sum(got.astype(F32), axis=0).astype(BF)


def spread_to(own, axes):
    count = lax.axis_size(axes)
    return lax.all_to_all(jnp.broadcast_to(own[None], (count,) + own.shape), axes, 0, 0)


STRIDES = {"x": 1, "y": 4, "z": 16}


def moved(a, by, axis_of_section):
    pairs = []
    for index, axis in enumerate(axis_of_section):
        stride = STRIDES[axis]
        for i in range(64):
            c = (i // stride) % 4
            to = i + ((c + by) % 4 - c) * stride
            pairs.append((index * 64 + i, index * 64 + to))
    return lax.ppermute(a, ("section", "dp"), pairs)


def stage(a, axis_of_section):
    one, three, two = [moved(a, by, axis_of_section) for by in (1, 3, 2)]
    return a, one, two, three


def total_of(arrays):
    return sum(a.astype(F32) for a in arrays).astype(BF)


def reduce_stage(pieces, axis_of_section):
    one, three, two = [moved(pieces[by], by, axis_of_section) for by in (1, 3, 2)]
    return total_of((pieces[0], one, two, three))


def tied(*arrays):
    return lax.optimization_barrier(arrays)


def per_device(
    images,
    queries,
    lengths,
    cotangent,
    encoder_project,
    encoder_output,
    encoder_expand,
    encoder_shrink,
    encoder_gain,
    encoder_shift,
    decoder_project,
    decoder_output,
    cross_query,
    cross_keyvalue,
    cross_output,
    decoder_expand,
    decoder_shrink,
    decoder_gain,
    decoder_shift,
):
    first = section() == 0
    chips = lax.axis_size("dp")
    chip = lax.axis_index("dp")

    def padded(a):
        return jnp.pad(jnp.where(first, a[0], a[1]), ((0, QP - QUERIES), (0, 0)))

    def added(a, b):
        return (a.astype(F32) + b.astype(F32)).astype(BF)

    keep, send, p, e, eo, deo, g1, r, wo_grad, dec_mine, dec_give = main(
        lengths, padded(queries), padded(cotangent),
        (encoder_gain, encoder_shift, decoder_gain, decoder_shift),
        images,
        (encoder_project, encoder_output, encoder_expand, encoder_shrink,
         decoder_project, decoder_output, cross_query, cross_keyvalue, cross_output,
         decoder_expand, decoder_shrink),
    )
    order = (2, 1, 3, 0)
    got = swapped(send)
    pieces = {k: added(keep[16 * k : 16 * (k + 1)], got[16 * k : 16 * (k + 1)]) for k in order}
    pieces[1], pieces[2], pieces[3], deo = tied(pieces[1], pieces[2], pieces[3], deo)
    received = [moved(pieces[k], k, "xy") for k in order[:3]]
    tail, img_keep, img_send = attention_back(
        e, eo, deo, r, wo_grad, p, images, g1, encoder_project
    )
    *received, tail = tied(*received, tail)
    everyone = ("section", "dp")
    tail_parts = scattered(tail.reshape(2 * chips, -1, LANES), everyone)
    img_got = swapped(img_send)
    dec_got = swapped(dec_give)
    bulk = total_of([pieces[0]] + received).reshape(4, 4, 96, D)
    bulk = reduce_stage([bulk[k] for k in range(4)], "yx")
    bulk = reduce_stage([bulk[k] for k in range(4)], "zz")
    bulk = jnp.stack(stage(bulk, "zz"))
    bulk = jnp.stack(stage(bulk, "yx"))
    bulk, tail_parts = tied(bulk, tail_parts)
    tail = spread_to(summed(tail_parts), everyone)
    own = list(stage(bulk, "xy"))
    images_out, decoded_out, queries_out = place(img_keep, img_got, dec_mine, dec_got)
    own[2], tail, images_out = tied(own[2], tail, images_out)
    project_out, output_out = unpack_tail(tail.reshape(8 * D, LANES))
    outs = unpack((chip // 16).reshape(1), own, [swapped(a) for a in own])
    return (
        decoded_out,
        images_out,
        queries_out,
        project_out,
        output_out,
        outs[7],
        outs[8],
        outs[11],
        outs[12],
        *outs[:7],
        outs[9],
        outs[10],
    )


def solution(mesh):
    over_images = P("dp", None, None)
    split = P("dp", None, "section")
    return jax.shard_map(
        per_device,
        mesh=mesh,
        in_specs=(over_images, over_images, P("dp"), over_images) + (P(),) * 15,
        out_specs=(split,) * 3 + (P(),) * 15,
        check_vma=False,
    )
```
